32 devices in a mesh: row: 8 (over y, x, core), col: 4 (over z).
Axes of the slice: x: 2, y: 2, z: 4, core: 2. Of those that a mesh axis runs over, the one named last changes fastest.
Arguments:
- amplitudes: bfloat16 [6144, 3072], P('row', 'col'), may hold values from -6 to 6
- integrals: bfloat16 [4, 768, 6144], P(None, 'row', 'col'), may hold values from -0.109375 to 0.109375
- residual_in: bfloat16 [6144, 6144], P('row', 'col'), may hold values from -3 to 3
- pair_class: int32 [64], P('row'), may hold values from 0 to 1
- cd_class: int32 [32], replicated, may hold values from 0 to 1
- ab_class: int32 [64], P('col'), may hold values from 0 to 1
Outputs:
- residual_out: bfloat16 [6144, 6144], P('row', 'col')
The draws below stay inside these ranges and needn't reach their ends.
All inputs are finite; a program needn't handle non-finite values.
Results may differ from the reference program's by a relative error of at most 0.001.
Values may be sent and summed in bfloat16 or wider, within the bound.
A program may use at most 128 MiB of HBM per device.

```python
import jax
import jax.numpy as jnp
from jax import lax

TILE = 96
PDEV = 768
K = 3072
GROUPS = 4
KG = 768
P_SIZE = 6144
M = 6144
N_ROW = 8


def set_ends(values, own_key, low, top_value):
    spot = [jax.random.randint(jax.random.fold_in(own_key, axis), (), 0, length) for axis, length in enumerate(values.shape)]
    longest = values.shape.index(max(values.shape))
    beside = spot[:longest] + [(spot[longest] + 1) % values.shape[longest]] + spot[longest + 1:]
    return values.at[tuple(spot)].set(low).at[tuple(beside)].set(top_value)


def steps_of(stream_key, extent, split, smallest, largest):
    level = 1.0
    for axis_at, parts in split:
        steps = jax.random.uniform(jax.random.fold_in(jax.random.fold_in(stream_key, 6), axis_at), (parts,), jnp.float32, smallest / len(split), largest / len(split))
        level = level * jnp.repeat(jnp.exp(steps), extent[axis_at] // parts).reshape((-1,) + (1,) * (len(extent) - 1 - axis_at))
    return level


def noise(stream_key, dims, scale, most, shards=(), dtype=jnp.bfloat16):
    array = scale * jax.random.normal(stream_key, dims, jnp.float32)
    if shards:
        array = array * steps_of(stream_key, dims, shards, -0.22, 0.18)
    return jnp.clip(array, -most, most).astype(dtype)


def setup_inputs(seed: int = 0) -> dict:
    key_list = jax.random.split(jax.random.key(seed), 7)
    amplitudes = noise(key_list[0], (P_SIZE, K), 1.0, 6.0, ((0, 8), (1, 4)))
    integrals = noise(key_list[1], (GROUPS, KG, M), K ** -0.5, 0.109375, ((1, 8), (2, 4)))
    residual_in = noise(key_list[2], (P_SIZE, M), 0.5, 3.0, ((0, 8), (1, 4)))
    pair_class = set_ends(jax.random.randint(key_list[3], (P_SIZE // TILE,), 0, 2), jax.random.fold_in(key_list[3], 1), 0, 1).astype(jnp.int32)
    cd_class = set_ends(jax.random.randint(key_list[4], (K // TILE,), 0, 2), jax.random.fold_in(key_list[4], 1), 0, 1).astype(jnp.int32)
    ab_class = set_ends(jax.random.randint(key_list[5], (M // TILE,), 0, 2), jax.random.fold_in(key_list[5], 1), 0, 1).astype(jnp.int32)
    return dict(amplitudes=amplitudes, integrals=integrals, residual_in=residual_in, pair_class=pair_class, cd_class=cd_class, ab_class=ab_class)


def reference(amplitudes, integrals, residual_in, pair_class, cd_class, ab_class):
    pair_labels = jnp.repeat(pair_class, TILE)
    cd_labels = jnp.repeat(cd_class, TILE)
    ab_labels = jnp.repeat(ab_class, TILE)
    nothing = jnp.zeros((), jnp.bfloat16)
    masked_amp = jnp.where(pair_labels[:, None] == cd_labels[None, :], amplitudes, nothing)
    flat_int = integrals.reshape(K, M)
    masked_int = jnp.where(cd_labels[:, None] == ab_labels[None, :], flat_int, nothing)

    def row_block(pair_item):
        amp_rows, prior_rows = pair_item
        ladder = jnp.dot(amp_rows, masked_int, preferred_element_type=jnp.float32)
        return (prior_rows.astype(jnp.float32) + ladder).astype(jnp.bfloat16)

    result = lax.map(row_block, (masked_amp.reshape(N_ROW, PDEV, K), residual_in.reshape(N_ROW, PDEV, M)))
    return result.reshape(P_SIZE, M)
```

```python
import functools

import jax
import jax.numpy as jnp
from jax import lax
from jax.experimental import pallas as pl
from jax.experimental.pallas import tpu as pltpu
from jax.sharding import PartitionSpec as P

TILE = 96
HALVES = 2
BLOCK = 256
MESH = pl.DeviceIdType.MESH


def kernel(pair_ref, cd_ref, pos_ref, ab_ref, amp_ref, int_ref, res_ref, out_ref,
           slabs, panel, masked, select, total, res_v,
           local_sem, int_send, int_recv, amp_send, amp_recv):
    r = lax.axis_index("row")
    z = lax.axis_index("col")
    last = 3
    core, x, y = lax.rem(r, 2), lax.rem(r // 2, 2), r // 4
    x_nbr, y_nbr, sib = r + 2 - 4 * x, r + 4 - 8 * y, r + 1 - 2 * core
    diag = y_nbr + 2 - 4 * x
    is_mid = jnp.logical_and(z > 0, z < last)
    groups, width, columns = panel.shape
    rows = amp_ref.shape[0]
    packed = slabs.shape[1]
    half = packed // HALVES

    barrier = pltpu.get_barrier_semaphore()
    for neighbour in (x_nbr, y_nbr, sib):
        pl.semaphore_signal(barrier, inc=1, device_id={"row": neighbour}, device_id_type=MESH)

    @pl.when(z > 0)
    def _():
        pl.semaphore_signal(barrier, inc=1, device_id={"col": z - 1}, device_id_type=MESH)

    @pl.when(z < last)
    def _():
        pl.semaphore_signal(barrier, inc=1, device_id={"col": z + 1}, device_id_type=MESH)

    def part(owner, g):
        span = pl.ds(pl.multiple_of(owner * TILE, TILE), TILE)
        return panel.at[:, span, :] if g is None else panel.at[g, span, :]

    def send_int(owner, g, send_at, recv_at, to, src=None):
        return pltpu.make_async_remote_copy(
            src_ref=part(owner, g) if src is None else src,
            dst_ref=part(owner, g),
            send_sem=int_send.at[send_at],
            recv_sem=int_recv.at[recv_at],
            device_id={"row": to},
            device_id_type=MESH,
        )

    def slab(j, h):
        return slabs.at[j, pl.ds(h * half, half), :]

    def send_amp(j, h, send_at, to):
        return pltpu.make_async_remote_copy(
            src_ref=slab(j, h),
            dst_ref=slab(j, h),
            send_sem=amp_send.at[send_at],
            recv_sem=amp_recv.at[j, h],
            device_id={"col": to},
            device_id_type=MESH,
        )

    own_x = [send_int(r, g, g, g, x_nbr, int_ref.at[g]) for g in range(4)]
    own_y = [send_int(r, g, 4 + g, 4 + g, y_nbr, int_ref.at[g]) for g in range(4)]
    own_sib = send_int(r, None, 8, 12, sib, int_ref)
    fwd_y = [send_int(x_nbr, g, 9 + g, 8 + g, y_nbr) for g in (0, 1)]
    fwd_x = [send_int(y_nbr, g, 9 + g, 8 + g, x_nbr) for g in (2, 3)]
    sib_x = send_int(x_nbr, None, 13, 13, sib)
    sib_y = send_int(y_nbr, None, 14, 14, sib)
    sib_d = send_int(diag, None, 15, 15, sib)
    keep = pltpu.make_async_copy(int_ref, part(r, None), local_sem.at[0])
    prior = pltpu.make_async_copy(res_ref, res_v, local_sem.at[1])

    def recv_int(owner, g, at):
        send_int(owner, g, 0, at, sib).wait_recv()

    pl.semaphore_wait(barrier, 3 + (z > 0).astype(jnp.int32) + (z < last).astype(jnp.int32))

    for copy in own_x + own_y:
        copy.start()
    own_sib.start()
    keep.start()
    prior.start()

    def fill_select(j):
        slot = lax.broadcasted_iota(jnp.int32, (packed, width), 0)
        select[...] = jnp.where(slot == pos_ref[j], 1.0, 0.0).astype(jnp.bfloat16)

    fill_select(z)

    @pl.loop(0, rows // BLOCK)
    def _(i):
        span = pl.ds(pl.multiple_of(i * BLOCK, BLOCK), BLOCK)
        kept = jnp.where(pair_ref[span, :] == cd_ref[z], amp_ref[span, :].astype(jnp.float32), 0.0)
        masked[span, :] = kept.astype(jnp.bfloat16)

    for h in range(HALVES):
        @pl.loop(0, rows // BLOCK)
        def _(i, h=h):
            span = pl.ds(pl.multiple_of(i * BLOCK, BLOCK), BLOCK)
            tile = lax.dot_general(
                select[pl.ds(h * half, half), :], masked[span, :],
                (((1,), (1,)), ((), ())), preferred_element_type=jnp.float32,
            )
            slabs[z, pl.ds(h * half, half), span] = tile.astype(jnp.bfloat16)

        @pl.when(z > 0)
        def _(h=h):
            send_amp(z, h, h, z - 1).start()

        @pl.when(z < last)
        def _(h=h):
            send_amp(z, h, 2 + h, z + 1).start()

    far = jnp.where(z == 1, 3, 0)
    far_to = jnp.where(z == 1, 0, 3)

    def pass_on(j, h, send_at, to):
        copy = send_amp(j, h, send_at, to)
        copy.wait_recv()
        copy.start()

    def pass_near(h):
        @pl.when(is_mid)
        def _():
            pass_on(z - 1, h, 4 + h, z + 1)
            pass_on(z + 1, h, 6 + h, z - 1)

    pass_near(0)
    for g in (0, 1):
        recv_int(x_nbr, g, g)
        fwd_y[g].start()
        recv_int(y_nbr, g, 4 + g)
    pass_near(1)
    for g in (2, 3):
        recv_int(y_nbr, g, 4 + g)
        fwd_x[g - 2].start()
        recv_int(x_nbr, g, g)
    sib_x.start()
    sib_y.start()

    @pl.when(is_mid)
    def _():
        for h in range(HALVES):
            pass_on(far, h, 8 + h, far_to)

    for g in range(4):
        recv_int(diag, g, 8 + g)
    sib_d.start()
    recv_int(sib, None, 12)
    recv_int(sib + 2 - 4 * x, None, 13)
    recv_int(sib + 4 - 8 * y, None, 14)
    recv_int(sib + 2 - 4 * x + 4 - 8 * y, None, 15)
    keep.wait()
    prior.wait()

    def add_slab(j, first):
        fill_select(j)

        @pl.loop(0, rows // BLOCK)
        def _(i):
            span = pl.ds(pl.multiple_of(i * BLOCK, BLOCK), BLOCK)
            spread = lax.dot_general(
                slabs[j, :, span], select[...],
                (((0,), (0,)), ((), ())), preferred_element_type=jnp.float32,
            )
            spread = jnp.where(pair_ref[span, :] == cd_ref[j], spread, 0.0).astype(jnp.bfloat16)
            part_sum = jnp.dot(spread, panel[j], preferred_element_type=jnp.float32)
            if first:
                total[span, :] = part_sum
            else:
                total[span, :] += part_sum

    add_slab(z, True)
    for step in (1, 2, 3):
        near = z - 1 if step == 1 else z + 1 if step == 2 else far
        j = jnp.where(z == 0, step, jnp.where(z == last, last - step, near))

        @pl.when(jnp.logical_not(is_mid))
        def _(j=j):
            for h in range(HALVES):
                send_amp(j, h, 0, 0).wait_recv()

        add_slab(j, False)

    @pl.loop(0, rows // BLOCK)
    def _(i):
        span = pl.ds(pl.multiple_of(i * BLOCK, BLOCK), BLOCK)
        ladder = jnp.where(pair_ref[span, :] == ab_ref[...], total[span, :], 0.0)
        out_ref[span, :] = (res_v[span, :].astype(jnp.float32) + ladder).astype(jnp.bfloat16)

    for copy in own_x + own_y + [own_sib] + fwd_y + fwd_x + [sib_x, sib_y, sib_d]:
        copy.wait_send()
    for h in range(HALVES):
        @pl.when(z > 0)
        def _(h=h):
            send_amp(z, h, h, z - 1).wait_send()

        @pl.when(z < last)
        def _(h=h):
            send_amp(z, h, 2 + h, z + 1).wait_send()

        @pl.when(is_mid)
        def _(h=h):
            send_amp(z - 1, h, 4 + h, z + 1).wait_send()
            send_amp(z + 1, h, 6 + h, z - 1).wait_send()
            send_amp(far, h, 8 + h, far_to).wait_send()


def call(slots, ident, pair_col, cd_rows, pos_rows, ab_row, amplitudes, integrals, residual_in):
    rows, width = amplitudes.shape
    groups, _, columns = integrals.shape
    vmem = pl.BlockSpec(memory_space=pltpu.VMEM)
    hbm = pl.BlockSpec(memory_space=pl.ANY)
    packed = slots * TILE
    return pl.pallas_call(
        kernel,
        out_shape=jax.ShapeDtypeStruct((rows, columns), jnp.bfloat16),
        in_specs=[vmem] * 5 + [hbm] * 2,
        out_specs=vmem,
        scratch_shapes=[
            pltpu.VMEM((groups, packed, rows), jnp.bfloat16),
            pltpu.VMEM((groups, width, columns), jnp.bfloat16),
            pltpu.VMEM((rows, width), jnp.bfloat16),
            pltpu.VMEM((packed, width), jnp.bfloat16),
            pltpu.VMEM((rows, columns), jnp.float32),
            pltpu.VMEM((rows, columns), jnp.bfloat16),
            pltpu.SemaphoreType.DMA((2,)),
            pltpu.SemaphoreType.DMA((16,)),
            pltpu.SemaphoreType.DMA((16,)),
            pltpu.SemaphoreType.DMA((10,)),
            pltpu.SemaphoreType.DMA((groups, HALVES)),
        ],
        compiler_params=pltpu.CompilerParams(
            collective_id=ident, has_side_effects=True, vmem_limit_bytes=48 * 1024 * 1024,
        ),
        cost_estimate=pl.CostEstimate(
            flops=2 * rows * width * groups * columns, bytes_accessed=2 * rows * columns * 3, transcendentals=0,
        ),
        name=f"ladder_{slots}",
    )(pair_col, cd_rows, pos_rows, ab_row, amplitudes, integrals, residual_in)


def paired(amplitudes, integrals, residual_in, pair_class, cd_class, ab_class):
    groups = integrals.shape[0]
    width = amplitudes.shape[1]
    per_group = width // TILE
    by_group = cd_class.reshape(groups, per_group)
    same = by_group[:, :, None] == by_group[:, None, :]
    before = jnp.arange(per_group)[None, :] < jnp.arange(per_group)[:, None]
    rank = jnp.sum((same & before[None]).astype(jnp.int32), axis=2)
    pos_rows = (rank[:, :, None] * TILE + jnp.arange(TILE)[None, None, :]).reshape(groups, 1, width)
    cd_rows = jnp.repeat(cd_class, TILE).reshape(groups, 1, width)
    pair_col = jnp.repeat(pair_class, TILE)[:, None]
    ab_row = jnp.repeat(ab_class, TILE)[None, :]
    operands = (pair_col, cd_rows, pos_rows, ab_row, amplitudes, integrals, residual_in)
    slots = jnp.max(rank) + 1
    sizes = (5, 6, 8)
    branches = [functools.partial(call, size, ident) for ident, size in enumerate(sizes)]
    which = sum((slots > size).astype(jnp.int32) for size in sizes[:-1])
    return lax.switch(which, branches, *operands)


def from_behind(value, axis, steps):
    count = lax.axis_size(axis)
    pairs = [(source, (source + steps) % count) for source in range(count)]
    return lax.ppermute(value, axis, pairs)


def ringed(amplitudes, integrals, residual_in, pair_class, cd_class, ab_class):
    pair_labels = jnp.repeat(pair_class, TILE)
    cd_labels = jnp.repeat(cd_class, TILE)
    ab_labels = jnp.repeat(ab_class, TILE)
    nothing = jnp.zeros((), jnp.bfloat16)
    slab_width = amplitudes.shape[1]

    def mask_amp(values, offset):
        labels = lax.dynamic_slice_in_dim(cd_labels, offset, values.shape[1])
        return jnp.where(pair_labels[:, None] == labels[None, :], values, nothing)

    def mask_int(values, offset):
        labels = lax.dynamic_slice_in_dim(cd_labels, offset, values.shape[0])
        return jnp.where(labels[:, None] == ab_labels[None, :], values, nothing)

    initial = residual_in.astype(jnp.float32)
    col_count = lax.axis_size("col")
    col_index = lax.axis_index("col")

    def contribute(ladder_sum, amp_slab, group_id):
        own_part = lax.dynamic_index_in_dim(integrals, group_id, 0, keepdims=False)
        int_panel = lax.all_gather(own_part, "row", axis=0, tiled=True)
        offset = group_id * slab_width
        return ladder_sum + jnp.dot(
            mask_amp(amp_slab, offset),
            mask_int(int_panel, offset),
            preferred_element_type=jnp.float32,
        )

    ladder_sum = contribute(initial, amplitudes, col_index)

    def advance(counter, state_pair):
        running, amp_slab = state_pair
        amp_slab = from_behind(amp_slab, "col", 1)
        group_id = (col_index - counter) % col_count
        return (contribute(running, amp_slab, group_id), amp_slab)

    ladder_sum, _ = lax.fori_loop(1, col_count, advance, (ladder_sum, amplitudes))
    return ladder_sum.astype(jnp.bfloat16)


def solution(mesh):
    local = paired if (mesh.shape["row"], mesh.shape["col"]) == (8, 4) else ringed
    return jax.shard_map(
        local,
        mesh=mesh,
        in_specs=(P("row", "col"), P(None, "row", "col"), P("row", "col"), P("row"), P(), P("col")),
        out_specs=P("row", "col"),
        check_vma=False,
    )
```

```python
import functools

import jax
import jax.numpy as jnp
from jax import lax
from jax.experimental import pallas as pl
from jax.experimental.pallas import tpu as pltpu
from jax.sharding import PartitionSpec as P

TILE = 96
HALVES = 2
BLOCK = 256
COLS = 512
MESH = pl.DeviceIdType.MESH


def kernel(pair_ref, cd_ref, ab_ref, amp_ref, int_ref, res_ref, out_ref,
           slabs, panel, paired_int, select, masked, total, res_v, pair_col, cd_col,
           local_sem, int_send, int_recv, amp_send, amp_recv):
    r = lax.axis_index("row")
    z = lax.axis_index("col")
    last = 3
    core, x, y = lax.rem(r, 2), lax.rem(r // 2, 2), r // 4
    x_nbr, y_nbr, sib = r + 2 - 4 * x, r + 4 - 8 * y, r + 1 - 2 * core
    diag = y_nbr + 2 - 4 * x
    is_mid = jnp.logical_and(z > 0, z < last)
    far = jnp.where(z == 1, 3, 0)
    far_to = jnp.where(z == 1, 0, 3)
    groups, width, columns = panel.shape
    tiles = width // TILE
    rows = amp_ref.shape[0]
    packed = slabs.shape[1]
    half = packed // HALVES
    order = [z]
    for step, near in ((1, z - 1), (2, z + 1), (3, far)):
        order.append(jnp.where(z == 0, step, jnp.where(z == last, last - step, near)))

    barrier = pltpu.get_barrier_semaphore()
    for neighbour in (x_nbr, y_nbr, sib):
        pl.semaphore_signal(barrier, inc=1, device_id={"row": neighbour}, device_id_type=MESH)

    @pl.when(z > 0)
    def _():
        pl.semaphore_signal(barrier, inc=1, device_id={"col": z - 1}, device_id_type=MESH)

    @pl.when(z < last)
    def _():
        pl.semaphore_signal(barrier, inc=1, device_id={"col": z + 1}, device_id_type=MESH)

    def rows_of(owner):
        return pl.ds(pl.multiple_of(owner * TILE, TILE), TILE)

    def send_int(owner, wave, kind, to, own=False, side=None):
        g = order[wave]
        if side is None:
            there = panel.at[g, rows_of(owner), :]
        else:
            there = panel.at[g, rows_of(owner), pl.ds(side * (columns // 2), columns // 2)]
        return pltpu.make_async_remote_copy(
            src_ref=int_ref.at[g] if own else there,
            dst_ref=there,
            send_sem=int_send.at[kind, wave],
            recv_sem=int_recv.at[kind, wave],
            device_id={"row": to},
            device_id_type=MESH,
        )

    def own_x(w):
        return send_int(r, w, 0, x_nbr, own=True)

    def own_y(w):
        return send_int(r, w, 1, y_nbr, own=True)

    def fwd_y(w):
        return send_int(x_nbr, w, 2, y_nbr, side=0)

    def fwd_x(w):
        return send_int(y_nbr, w, 3, x_nbr, side=1)

    def to_sib(w, kind):
        return send_int((r, x_nbr, y_nbr, diag)[kind - 4], w, kind, sib, own=kind == 4)

    def recv_int(w, kind):
        owner = (x_nbr, y_nbr, diag, diag, sib, sib + 2 - 4 * x, sib + 4 - 8 * y, sib + 2 - 4 * x + 4 - 8 * y)[kind]
        send_int(owner, w, kind, sib, side={2: 0, 3: 1}.get(kind)).wait_recv()

    def slab(j, h):
        return slabs.at[j, pl.ds(h * half, half), :]

    def send_amp(j, h, send_at, to):
        return pltpu.make_async_remote_copy(
            src_ref=slab(j, h),
            dst_ref=slab(j, h),
            send_sem=amp_send.at[send_at],
            recv_sem=amp_recv.at[j, h],
            device_id={"col": to},
            device_id_type=MESH,
        )

    keep = pltpu.make_async_copy(int_ref, panel.at[:, rows_of(r), :], local_sem.at[0])
    prior = pltpu.make_async_copy(res_ref, res_v, local_sem.at[1])

    pl.semaphore_wait(barrier, 3 + (z > 0).astype(jnp.int32) + (z < last).astype(jnp.int32))

    for w in (0, 1):
        own_x(w).start()
        own_y(w).start()
    keep.start()

    def lane_labels(ref, base, count):
        lane = lax.broadcasted_iota(jnp.int32, (1, count * TILE), 1)
        labels = jnp.zeros_like(lane)
        for t in range(count):
            labels = jnp.where(lane >= t * TILE, ref[base + t], labels)
        return labels

    def fill_select(j):
        lane = lax.broadcasted_iota(jnp.int32, (1, width), 1)
        place = jnp.zeros_like(lane)
        ones = jnp.int32(0)
        for t in range(tiles):
            label = cd_ref[j * tiles + t]
            rank = jnp.where(label == 1, ones, t - ones)
            place = jnp.where(lane >= t * TILE, lane + (rank - t) * TILE, place)
            ones = ones + label
        slot = lax.broadcasted_iota(jnp.int32, (packed, width), 0)
        select[...] = jnp.where(slot == place, 1.0, 0.0).astype(jnp.bfloat16)

    for t in range(rows // TILE):
        pair_col[pl.ds(t * TILE, TILE), :] = jnp.full((TILE, 1), pair_ref[t], jnp.int32)
    fill_select(z)
    own_labels = lane_labels(cd_ref, z * tiles, tiles)

    @pl.loop(0, rows // BLOCK)
    def _(i):
        span = pl.ds(pl.multiple_of(i * BLOCK, BLOCK), BLOCK)
        kept = jnp.where(pair_col[span, :] == own_labels, amp_ref[span, :].astype(jnp.float32), 0.0)
        masked[span, :] = kept.astype(jnp.bfloat16)

    for h in range(HALVES):
        @pl.loop(0, rows // BLOCK)
        def _(i, h=h):
            span = pl.ds(pl.multiple_of(i * BLOCK, BLOCK), BLOCK)
            tile = lax.dot_general(
                select[pl.ds(h * half, half), :], masked[span, :],
                (((1,), (1,)), ((), ())), preferred_element_type=jnp.float32,
            )
            slabs[z, pl.ds(h * half, half), span] = tile.astype(jnp.bfloat16)

        @pl.when(z > 0)
        def _(h=h):
            send_amp(z, h, h, z - 1).start()

        @pl.when(z < last)
        def _(h=h):
            send_amp(z, h, 2 + h, z + 1).start()

    for w in range(groups):
        to_sib(w, 4).start()
    prior.start()
    for g in range(groups):
        for t in range(tiles):
            cd_col[g, pl.ds(t * TILE, TILE), :] = jnp.full((TILE, 1), cd_ref[g * tiles + t], jnp.int32)
    ab_labels = lane_labels(ab_ref, 0, columns // TILE)

    def pass_on(j, h, send_at, to):
        copy = send_amp(j, h, send_at, to)
        copy.wait_recv()
        copy.start()

    def pass_near(h):
        @pl.when(is_mid)
        def _():
            pass_on(z - 1, h, 4 + h, z + 1)
            pass_on(z + 1, h, 6 + h, z - 1)

    def pass_far(h):
        @pl.when(is_mid)
        def _():
            pass_on(far, h, 8 + h, far_to)

    def take_wave(w):
        recv_int(w, 0)
        fwd_y(w).start()
        recv_int(w, 1)
        fwd_x(w).start()
        if w + 2 < groups:
            own_x(w + 2).start()
            own_y(w + 2).start()
        to_sib(w, 5).start()
        to_sib(w, 6).start()

    def take_diag(w):
        recv_int(w, 2)
        recv_int(w, 3)
        to_sib(w, 7).start()

    def pair_up(w):
        j = order[w]
        if w == 0:
            keep.wait()
        for kind in (4, 5, 6, 7):
            recv_int(w, kind)
        fill_select(j)
        for c in range(columns // COLS):
            at = slice(c * COLS, (c + 1) * COLS)
            part = jnp.where(cd_col[j] == ab_labels[:, at], panel[j, :, at].astype(jnp.float32), 0.0)
            paired_int[:, at] = jnp.dot(
                select[...], part.astype(jnp.bfloat16), preferred_element_type=jnp.float32
            ).astype(jnp.bfloat16)

    def wait_amp(w, h):
        @pl.when(jnp.logical_not(is_mid))
        def _():
            send_amp(order[w], h, 0, 0).wait_recv()

    def product(w, span, start, size):
        return lax.dot_general(
            slabs[order[w], pl.ds(start, size), span], paired_int[pl.ds(start, size), :],
            (((0,), (0,)), ((), ())), preferred_element_type=jnp.float32,
        )

    def multiply(w, start, size):
        @pl.loop(0, rows // BLOCK)
        def _(i):
            span = pl.ds(pl.multiple_of(i * BLOCK, BLOCK), BLOCK)
            if w == 0:
                total[span, :] = product(w, span, start, size)
            else:
                total[span, :] += product(w, span, start, size)

    pass_near(0)
    take_wave(0)
    pass_near(1)
    take_wave(1)
    take_diag(0)
    pair_up(0)
    multiply(0, 0, packed)
    pass_far(0)
    take_wave(2)
    take_diag(1)
    pair_up(1)
    for h in range(HALVES):
        wait_amp(1, h)
    multiply(1, 0, packed)
    pass_far(1)
    take_wave(3)
    take_diag(2)
    pair_up(2)
    for h in range(HALVES):
        wait_amp(2, h)
    multiply(2, 0, packed)
    take_diag(3)
    pair_up(3)
    wait_amp(3, 0)
    multiply(3, 0, half)
    prior.wait()
    wait_amp(3, 1)

    @pl.loop(0, rows // BLOCK)
    def _(i):
        span = pl.ds(pl.multiple_of(i * BLOCK, BLOCK), BLOCK)
        ladder = total[span, :] + product(3, span, half, half)
        ladder = jnp.where(pair_col[span, :] == ab_labels, ladder, 0.0)
        out_ref[span, :] = (res_v[span, :].astype(jnp.float32) + ladder).astype(jnp.bfloat16)

    for w in range(groups):
        for copy in (own_x, own_y, fwd_y, fwd_x):
            copy(w).wait_send()
        for kind in (4, 5, 6, 7):
            to_sib(w, kind).wait_send()
    for h in range(HALVES):
        @pl.when(z > 0)
        def _(h=h):
            send_amp(z, h, h, z - 1).wait_send()

        @pl.when(z < last)
        def _(h=h):
            send_amp(z, h, 2 + h, z + 1).wait_send()

        @pl.when(is_mid)
        def _(h=h):
            send_amp(z - 1, h, 4 + h, z + 1).wait_send()
            send_amp(z + 1, h, 6 + h, z - 1).wait_send()
            send_amp(far, h, 8 + h, far_to).wait_send()


def call(slots, ident, pair_class, cd_class, ab_class, amplitudes, integrals, residual_in):
    rows, width = amplitudes.shape
    groups, _, columns = integrals.shape
    smem = pl.BlockSpec(memory_space=pltpu.SMEM)
    vmem = pl.BlockSpec(memory_space=pltpu.VMEM)
    hbm = pl.BlockSpec(memory_space=pl.ANY)
    packed = slots * TILE
    return pl.pallas_call(
        kernel,
        out_shape=jax.ShapeDtypeStruct((rows, columns), jnp.bfloat16),
        in_specs=[smem] * 3 + [vmem] + [hbm] * 2,
        out_specs=vmem,
        scratch_shapes=[
            pltpu.VMEM((groups, packed, rows), jnp.bfloat16),
            pltpu.VMEM((groups, width, columns), jnp.bfloat16),
            pltpu.VMEM((packed, columns), jnp.bfloat16),
            pltpu.VMEM((packed, width), jnp.bfloat16),
            pltpu.VMEM((rows, width), jnp.bfloat16),
            pltpu.VMEM((rows, columns), jnp.float32),
            pltpu.VMEM((rows, columns), jnp.bfloat16),
            pltpu.VMEM((rows, 1), jnp.int32),
            pltpu.VMEM((groups, width, 1), jnp.int32),
            pltpu.SemaphoreType.DMA((2,)),
            pltpu.SemaphoreType.DMA((8, groups)),
            pltpu.SemaphoreType.DMA((8, groups)),
            pltpu.SemaphoreType.DMA((10,)),
            pltpu.SemaphoreType.DMA((groups, HALVES)),
        ],
        compiler_params=pltpu.CompilerParams(
            collective_id=ident, has_side_effects=True, vmem_limit_bytes=48 * 1024 * 1024,
        ),
        cost_estimate=pl.CostEstimate(
            flops=2 * rows * width * groups * columns, bytes_accessed=2 * rows * columns * 3, transcendentals=0,
        ),
        name=f"ladder_{slots}",
    )(pair_class, cd_class, ab_class, amplitudes, integrals, residual_in)


def paired(amplitudes, integrals, residual_in, pair_class, cd_class, ab_class):
    groups = integrals.shape[0]
    per_group = amplitudes.shape[1] // TILE
    ones = jnp.sum(cd_class.reshape(groups, per_group), axis=1)
    slots = jnp.max(jnp.maximum(ones, per_group - ones))
    sizes = (5, 6, 7, 8)
    branches = [functools.partial(call, size, ident) for ident, size in enumerate(sizes)]
    which = jnp.clip(slots - sizes[0], 0, len(sizes) - 1)
    return lax.switch(which, branches, pair_class, cd_class, ab_class, amplitudes, integrals, residual_in)


def from_behind(value, axis, steps):
    count = lax.axis_size(axis)
    pairs = [(source, (source + steps) % count) for source in range(count)]
    return lax.ppermute(value, axis, pairs)


def ringed(amplitudes, integrals, residual_in, pair_class, cd_class, ab_class):
    pair_labels = jnp.repeat(pair_class, TILE)
    cd_labels = jnp.repeat(cd_class, TILE)
    ab_labels = jnp.repeat(ab_class, TILE)
    nothing = jnp.zeros((), jnp.bfloat16)
    slab_width = amplitudes.shape[1]

    def mask_amp(values, offset):
        labels = lax.dynamic_slice_in_dim(cd_labels, offset, values.shape[1])
        return jnp.where(pair_labels[:, None] == labels[None, :], values, nothing)

    def mask_int(values, offset):
        labels = lax.dynamic_slice_in_dim(cd_labels, offset, values.shape[0])
        return jnp.where(labels[:, None] == ab_labels[None, :], values, nothing)

    initial = residual_in.astype(jnp.float32)
    col_count = lax.axis_size("col")
    col_index = lax.axis_index("col")

    def contribute(ladder_sum, amp_slab, group_id):
        own_part = lax.dynamic_index_in_dim(integrals, group_id, 0, keepdims=False)
        int_panel = lax.all_gather(own_part, "row", axis=0, tiled=True)
        offset = group_id * slab_width
        return ladder_sum + jnp.dot(
            mask_amp(amp_slab, offset),
            mask_int(int_panel, offset),
            preferred_element_type=jnp.float32,
        )

    ladder_sum = contribute(initial, amplitudes, col_index)

    def advance(counter, state_pair):
        running, amp_slab = state_pair
        amp_slab = from_behind(amp_slab, "col", 1)
        group_id = (col_index - counter) % col_count
        return (contribute(running, amp_slab, group_id), amp_slab)

    ladder_sum, _ = lax.fori_loop(1, col_count, advance, (ladder_sum, amplitudes))
    return ladder_sum.astype(jnp.bfloat16)


def solution(mesh):
    local = paired if (mesh.shape["row"], mesh.shape["col"]) == (8, 4) else ringed
    return jax.shard_map(
        local,
        mesh=mesh,
        in_specs=(P("row", "col"), P(None, "row", "col"), P("row", "col"), P("row"), P(), P("col")),
        out_specs=P("row", "col"),
        check_vma=False,
    )
```

```python
import functools

import jax
import jax.numpy as jnp
from jax import lax
from jax.experimental import pallas as pl
from jax.experimental.pallas import tpu as pltpu
from jax.sharding import PartitionSpec as P

TILE = 96
HALVES = 2
BLOCK = 256
COLS = 512
MESH = pl.DeviceIdType.MESH


def kernel(pair_ref, cd_ref, ab_ref, amp_ref, int_ref, res_ref, out_ref,
           slabs, panel, paired_int, select, masked, total, res_v, pair_col, cd_col, ab_lane,
           local_sem, int_send, int_recv, amp_send, amp_recv):
    r = lax.axis_index("row")
    z = lax.axis_index("col")
    last = 3
    core, x, y = lax.rem(r, 2), lax.rem(r // 2, 2), r // 4
    x_nbr, y_nbr, sib = r + 2 - 4 * x, r + 4 - 8 * y, r + 1 - 2 * core
    diag = y_nbr + 2 - 4 * x
    is_mid = jnp.logical_and(z > 0, z < last)
    far = jnp.where(z == 1, 3, 0)
    far_to = jnp.where(z == 1, 0, 3)
    groups, width, columns = panel.shape
    tiles = width // TILE
    rows = amp_ref.shape[0]
    packed = slabs.shape[1]
    half = packed // HALVES
    def order(w):
        near = jnp.where(w == 1, z - 1, jnp.where(w == 2, z + 1, far))
        there = jnp.where(z == 0, w, jnp.where(z == last, last - w, near))
        return jnp.where(w == 0, z, there)

    barrier = pltpu.get_barrier_semaphore()
    for neighbour in (x_nbr, y_nbr, sib):
        pl.semaphore_signal(barrier, inc=1, device_id={"row": neighbour}, device_id_type=MESH)

    @pl.when(z > 0)
    def _():
        pl.semaphore_signal(barrier, inc=1, device_id={"col": z - 1}, device_id_type=MESH)

    @pl.when(z < last)
    def _():
        pl.semaphore_signal(barrier, inc=1, device_id={"col": z + 1}, device_id_type=MESH)

    def rows_of(owner):
        return pl.ds(pl.multiple_of(owner * TILE, TILE), TILE)

    def send_int(owner, wave, kind, to, own=False, side=None):
        g = order(wave)
        if side is None:
            there = panel.at[g, rows_of(owner), :]
        else:
            there = panel.at[g, rows_of(owner), pl.ds(side * (columns // 2), columns // 2)]
        return pltpu.make_async_remote_copy(
            src_ref=int_ref.at[g] if own else there,
            dst_ref=there,
            send_sem=int_send.at[kind, wave],
            recv_sem=int_recv.at[kind, wave],
            device_id={"row": to},
            device_id_type=MESH,
        )

    def own_x(w):
        return send_int(r, w, 0, x_nbr, own=True)

    def own_y(w):
        return send_int(r, w, 1, y_nbr, own=True)

    def fwd_y(w):
        return send_int(x_nbr, w, 2, y_nbr, side=0)

    def fwd_x(w):
        return send_int(y_nbr, w, 3, x_nbr, side=1)

    def to_sib(w, kind):
        return send_int((r, x_nbr, y_nbr, diag)[kind - 4], w, kind, sib, own=kind == 4)

    def recv_int(w, kind):
        owner = (x_nbr, y_nbr, diag, diag, sib, sib + 2 - 4 * x, sib + 4 - 8 * y, sib + 2 - 4 * x + 4 - 8 * y)[kind]
        send_int(owner, w, kind, sib, side={2: 0, 3: 1}.get(kind)).wait_recv()

    def slab(j, h):
        return slabs.at[j, pl.ds(pl.multiple_of(h * half, 16), half), :]

    def send_amp(j, h, send_at, to):
        return pltpu.make_async_remote_copy(
            src_ref=slab(j, h),
            dst_ref=slab(j, h),
            send_sem=amp_send.at[send_at],
            recv_sem=amp_recv.at[j, h],
            device_id={"col": to},
            device_id_type=MESH,
        )

    keep = pltpu.make_async_copy(int_ref, panel.at[:, rows_of(r), :], local_sem.at[0])
    prior = pltpu.make_async_copy(res_ref, res_v, local_sem.at[1])

    pl.semaphore_wait(barrier, 3 + (z > 0).astype(jnp.int32) + (z < last).astype(jnp.int32))

    for w in (0, 1):
        own_x(w).start()
        own_y(w).start()
    keep.start()

    def lane_labels(ref, base, count):
        lane = lax.broadcasted_iota(jnp.int32, (1, count * TILE), 1)
        labels = jnp.zeros_like(lane)
        for t in range(count):
            labels = jnp.where(lane >= t * TILE, ref[base + t], labels)
        return labels

    def fill_select(j):
        lane = lax.broadcasted_iota(jnp.int32, (1, width), 1)
        place = jnp.zeros_like(lane)
        ones = jnp.int32(0)
        for t in range(tiles):
            label = cd_ref[j * tiles + t]
            rank = jnp.where(label == 1, ones, t - ones)
            place = jnp.where(lane >= t * TILE, lane + (rank - t) * TILE, place)
            ones = ones + label
        slot = lax.broadcasted_iota(jnp.int32, (packed, width), 0)
        select[...] = jnp.where(slot == place, 1.0, 0.0).astype(jnp.bfloat16)

    for t in range(rows // TILE):
        pair_col[pl.ds(t * TILE, TILE), :] = jnp.full((TILE, 1), pair_ref[t], jnp.int32)
    fill_select(z)
    own_labels = lane_labels(cd_ref, z * tiles, tiles)

    @pl.loop(0, rows // BLOCK)
    def _(i):
        span = pl.ds(pl.multiple_of(i * BLOCK, BLOCK), BLOCK)
        kept = jnp.where(pair_col[span, :] == own_labels, amp_ref[span, :].astype(jnp.float32), 0.0)
        masked[span, :] = kept.astype(jnp.bfloat16)

    for h in range(HALVES):
        @pl.loop(0, rows // BLOCK)
        def _(i, h=h):
            span = pl.ds(pl.multiple_of(i * BLOCK, BLOCK), BLOCK)
            tile = lax.dot_general(
                select[pl.ds(h * half, half), :], masked[span, :],
                (((1,), (1,)), ((), ())), preferred_element_type=jnp.float32,
            )
            slabs[z, pl.ds(h * half, half), span] = tile.astype(jnp.bfloat16)

        @pl.when(z > 0)
        def _(h=h):
            send_amp(z, h, h, z - 1).start()

        @pl.when(z < last)
        def _(h=h):
            send_amp(z, h, 2 + h, z + 1).start()

    for w in range(groups):
        to_sib(w, 4).start()
    prior.start()
    for g in range(groups):
        for t in range(tiles):
            cd_col[g, pl.ds(t * TILE, TILE), :] = jnp.full((TILE, 1), cd_ref[g * tiles + t], jnp.int32)
    ab_lane[...] = lane_labels(ab_ref, 0, columns // TILE)

    def pass_on(j, h, send_at, to):
        copy = send_amp(j, h, send_at, to)
        copy.wait_recv()
        copy.start()

    def pass_near(h):
        @pl.when(is_mid)
        def _():
            pass_on(z - 1, h, 4 + h, z + 1)
            pass_on(z + 1, h, 6 + h, z - 1)

    def pass_far(h):
        @pl.when(is_mid)
        def _():
            pass_on(far, h, 8 + h, far_to)

    def take_wave(w):
        recv_int(w, 0)
        fwd_y(w).start()
        recv_int(w, 1)
        fwd_x(w).start()

        @pl.when(w + 2 < groups)
        def _():
            own_x(w + 2).start()
            own_y(w + 2).start()

        to_sib(w, 5).start()
        to_sib(w, 6).start()

    def take_diag(w):
        recv_int(w, 2)
        recv_int(w, 3)
        to_sib(w, 7).start()

    def pair_up(w):
        j = order(w)
        for kind in (4, 5, 6, 7):
            recv_int(w, kind)
        fill_select(j)

        @pl.loop(0, columns // COLS)
        def _(c):
            at = pl.ds(pl.multiple_of(c * COLS, COLS), COLS)
            part = jnp.where(cd_col[j] == ab_lane[:, at], panel[j, :, at].astype(jnp.float32), 0.0)
            paired_int[:, at] = jnp.dot(
                select[...], part.astype(jnp.bfloat16), preferred_element_type=jnp.float32
            ).astype(jnp.bfloat16)

    def wait_amp(w, h):
        @pl.when(jnp.logical_not(is_mid))
        def _():
            send_amp(order(w), h, 0, 0).wait_recv()

    def multiply(w, start, size, store):
        @pl.loop(0, rows // BLOCK)
        def _(i):
            span = pl.ds(pl.multiple_of(i * BLOCK, BLOCK), BLOCK)
            left = slabs[order(w), pl.ds(start, size), span].T

            @pl.loop(0, columns // COLS)
            def _(c):
                at = pl.ds(pl.multiple_of(c * COLS, COLS), COLS)
                store(span, at, jnp.dot(left, paired_int[pl.ds(start, size), at], preferred_element_type=jnp.float32))

    def add(span, at, value):
        total[span, at] += value

    def finish(span, at, value):
        ladder = jnp.where(pair_col[span, :] == ab_lane[:, at], total[span, at] + value, 0.0)
        out_ref[span, at] = (res_v[span, at].astype(jnp.float32) + ladder).astype(jnp.bfloat16)

    total[...] = jnp.zeros_like(total)
    pass_near(0)
    take_wave(0)
    pass_near(1)
    keep.wait()

    @pl.loop(0, groups - 1)
    def _(w):
        @pl.when(w > 0)
        def _():
            pass_far(w - 1)

        take_wave(w + 1)
        take_diag(w)
        pair_up(w)

        @pl.when(w > 0)
        def _():
            for h in range(HALVES):
                wait_amp(w, h)

        multiply(w, 0, packed, add)

    take_diag(last)
    pair_up(last)
    wait_amp(last, 0)
    multiply(last, 0, half, add)
    prior.wait()
    wait_amp(last, 1)
    multiply(last, half, half, finish)

    for w in range(groups):
        for copy in (own_x, own_y, fwd_y, fwd_x):
            copy(w).wait_send()
        for kind in (4, 5, 6, 7):
            to_sib(w, kind).wait_send()
    for h in range(HALVES):
        @pl.when(z > 0)
        def _(h=h):
            send_amp(z, h, h, z - 1).wait_send()

        @pl.when(z < last)
        def _(h=h):
            send_amp(z, h, 2 + h, z + 1).wait_send()

        @pl.when(is_mid)
        def _(h=h):
            send_amp(z - 1, h, 4 + h, z + 1).wait_send()
            send_amp(z + 1, h, 6 + h, z - 1).wait_send()
            send_amp(far, h, 8 + h, far_to).wait_send()


def call(slots, ident, pair_class, cd_class, ab_class, amplitudes, integrals, residual_in):
    rows, width = amplitudes.shape
    groups, _, columns = integrals.shape
    smem = pl.BlockSpec(memory_space=pltpu.SMEM)
    vmem = pl.BlockSpec(memory_space=pltpu.VMEM)
    hbm = pl.BlockSpec(memory_space=pl.ANY)
    packed = slots * TILE
    return pl.pallas_call(
        kernel,
        out_shape=jax.ShapeDtypeStruct((rows, columns), jnp.bfloat16),
        in_specs=[smem] * 3 + [vmem] + [hbm] * 2,
        out_specs=vmem,
        scratch_shapes=[
            pltpu.VMEM((groups, packed, rows), jnp.bfloat16),
            pltpu.VMEM((groups, width, columns), jnp.bfloat16),
            pltpu.VMEM((packed, columns), jnp.bfloat16),
            pltpu.VMEM((packed, width), jnp.bfloat16),
            pltpu.VMEM((rows, width), jnp.bfloat16),
            pltpu.VMEM((rows, columns), jnp.float32),
            pltpu.VMEM((rows, columns), jnp.bfloat16),
            pltpu.VMEM((rows, 1), jnp.int32),
            pltpu.VMEM((groups, width, 1), jnp.int32),
            pltpu.VMEM((1, columns), jnp.int32),
            pltpu.SemaphoreType.DMA((2,)),
            pltpu.SemaphoreType.DMA((8, groups)),
            pltpu.SemaphoreType.DMA((8, groups)),
            pltpu.SemaphoreType.DMA((10,)),
            pltpu.SemaphoreType.DMA((groups, HALVES)),
        ],
        compiler_params=pltpu.CompilerParams(
            collective_id=ident, has_side_effects=True, vmem_limit_bytes=48 * 1024 * 1024,
        ),
        cost_estimate=pl.CostEstimate(
            flops=2 * rows * width * groups * columns, bytes_accessed=2 * rows * columns * 3, transcendentals=0,
        ),
        name=f"ladder_{slots}",
    )(pair_class, cd_class, ab_class, amplitudes, integrals, residual_in)


def paired(amplitudes, integrals, residual_in, pair_class, cd_class, ab_class):
    groups = integrals.shape[0]
    per_group = amplitudes.shape[1] // TILE
    ones = jnp.sum(cd_class.reshape(groups, per_group), axis=1)
    slots = jnp.max(jnp.maximum(ones, per_group - ones))
    sizes = (5, 6, 7, 8)
    branches = [functools.partial(call, size, ident) for ident, size in enumerate(sizes)]
    which = jnp.clip(slots - sizes[0], 0, len(sizes) - 1)
    return lax.switch(which, branches, pair_class, cd_class, ab_class, amplitudes, integrals, residual_in)


def from_behind(value, axis, steps):
    count = lax.axis_size(axis)
    pairs = [(source, (source + steps) % count) for source in range(count)]
    return lax.ppermute(value, axis, pairs)


def ringed(amplitudes, integrals, residual_in, pair_class, cd_class, ab_class):
    pair_labels = jnp.repeat(pair_class, TILE)
    cd_labels = jnp.repeat(cd_class, TILE)
    ab_labels = jnp.repeat(ab_class, TILE)
    nothing = jnp.zeros((), jnp.bfloat16)
    slab_width = amplitudes.shape[1]

    def mask_amp(values, offset):
        labels = lax.dynamic_slice_in_dim(cd_labels, offset, values.shape[1])
        return jnp.where(pair_labels[:, None] == labels[None, :], values, nothing)

    def mask_int(values, offset):
        labels = lax.dynamic_slice_in_dim(cd_labels, offset, values.shape[0])
        return jnp.where(labels[:, None] == ab_labels[None, :], values, nothing)

    initial = residual_in.astype(jnp.float32)
    col_count = lax.axis_size("col")
    col_index = lax.axis_index("col")

    def contribute(ladder_sum, amp_slab, group_id):
        own_part = lax.dynamic_index_in_dim(integrals, group_id, 0, keepdims=False)
        int_panel = lax.all_gather(own_part, "row", axis=0, tiled=True)
        offset = group_id * slab_width
        return ladder_sum + jnp.dot(
            mask_amp(amp_slab, offset),
            mask_int(int_panel, offset),
            preferred_element_type=jnp.float32,
        )

    ladder_sum = contribute(initial, amplitudes, col_index)

    def advance(counter, state_pair):
        running, amp_slab = state_pair
        amp_slab = from_behind(amp_slab, "col", 1)
        group_id = (col_index - counter) % col_count
        return (contribute(running, amp_slab, group_id), amp_slab)

    ladder_sum, _ = lax.fori_loop(1, col_count, advance, (ladder_sum, amplitudes))
    return ladder_sum.astype(jnp.bfloat16)


def solution(mesh):
    local = paired if (mesh.shape["row"], mesh.shape["col"]) == (8, 4) else ringed
    return jax.shard_map(
        local,
        mesh=mesh,
        in_specs=(P("row", "col"), P(None, "row", "col"), P("row", "col"), P("row"), P(), P("col")),
        out_specs=P("row", "col"),
        check_vma=False,
    )
```

```python
import functools

import jax
import jax.numpy as jnp
from jax import lax
from jax.experimental import pallas as pl
from jax.experimental.pallas import tpu as pltpu
from jax.sharding import PartitionSpec as P

TILE = 96
HALVES = 2
BASE = 4
BLOCK = 256
COLS = 512
MESH = pl.DeviceIdType.MESH


def kernel(pair_ref, cd_ref, ab_ref, amp_ref, int_ref, res_ref, out_ref,
           slabs, pool_in, pool_out, pool_int, pool_select, panel, paired_int, select, masked, total, res_v, pair_col, cd_col, ab_lane,
           local_sem, int_send, int_recv, amp_send, amp_recv, pool_send, pool_recv):
    r = lax.axis_index("row")
    z = lax.axis_index("col")
    last = 3
    core, x, y = lax.rem(r, 2), lax.rem(r // 2, 2), r // 4
    x_nbr, y_nbr, sib = r + 2 - 4 * x, r + 4 - 8 * y, r + 1 - 2 * core
    diag = y_nbr + 2 - 4 * x
    is_mid = jnp.logical_and(z > 0, z < last)
    far = jnp.where(z == 1, 3, 0)
    far_to = jnp.where(z == 1, 0, 3)
    groups, width, columns = panel.shape
    tiles = width // TILE
    rows = amp_ref.shape[0]
    packed = slabs.shape[1]
    half = packed // HALVES
    pooled = pool_in.shape[1]
    cols = COLS if pooled <= COLS else COLS // 2
    def order(w):
        near = jnp.where(w == 1, z - 1, jnp.where(w == 2, z + 1, far))
        there = jnp.where(z == 0, w, jnp.where(z == last, last - w, near))
        return jnp.where(w == 0, z, there)

    barrier = pltpu.get_barrier_semaphore()
    for neighbour in (x_nbr, y_nbr, sib):
        pl.semaphore_signal(barrier, inc=1, device_id={"row": neighbour}, device_id_type=MESH)

    @pl.when(z > 0)
    def _():
        pl.semaphore_signal(barrier, inc=1, device_id={"col": z - 1}, device_id_type=MESH)

    @pl.when(z < last)
    def _():
        pl.semaphore_signal(barrier, inc=1, device_id={"col": z + 1}, device_id_type=MESH)

    def rows_of(owner):
        return pl.ds(pl.multiple_of(owner * TILE, TILE), TILE)

    def send_int(owner, wave, kind, to, own=False, side=None):
        g = order(wave)
        if side is None:
            there = panel.at[g, rows_of(owner), :]
        else:
            there = panel.at[g, rows_of(owner), pl.ds(side * (columns // 2), columns // 2)]
        return pltpu.make_async_remote_copy(
            src_ref=int_ref.at[g] if own else there,
            dst_ref=there,
            send_sem=int_send.at[kind, wave],
            recv_sem=int_recv.at[kind, wave],
            device_id={"row": to},
            device_id_type=MESH,
        )

    def own_x(w):
        return send_int(r, w, 0, x_nbr, own=True)

    def own_y(w):
        return send_int(r, w, 1, y_nbr, own=True)

    def fwd_y(w):
        return send_int(x_nbr, w, 2, y_nbr, side=0)

    def fwd_x(w):
        return send_int(y_nbr, w, 3, x_nbr, side=1)

    def to_sib(w, kind):
        return send_int((r, x_nbr, y_nbr, diag)[kind - 4], w, kind, sib, own=kind == 4)

    def recv_int(w, kind):
        owner = (x_nbr, y_nbr, diag, diag, sib, sib + 2 - 4 * x, sib + 4 - 8 * y, sib + 2 - 4 * x + 4 - 8 * y)[kind]
        send_int(owner, w, kind, sib, side={2: 0, 3: 1}.get(kind)).wait_recv()

    def slab(j, h):
        return slabs.at[j, pl.ds(pl.multiple_of(h * half, 16), half), :]

    def send_amp(j, h, send_at, to):
        return pltpu.make_async_remote_copy(
            src_ref=slab(j, h),
            dst_ref=slab(j, h),
            send_sem=amp_send.at[send_at],
            recv_sem=amp_recv.at[j, h],
            device_id={"col": to},
            device_id_type=MESH,
        )

    keep = pltpu.make_async_copy(int_ref, panel.at[:, rows_of(r), :], local_sem.at[0])
    prior = pltpu.make_async_copy(res_ref, res_v, local_sem.at[1])

    pl.semaphore_wait(barrier, 3 + (z > 0).astype(jnp.int32) + (z < last).astype(jnp.int32))

    for w in (0, 1):
        own_x(w).start()
        own_y(w).start()
    keep.start()

    def lane_labels(ref, base, count):
        lane = lax.broadcasted_iota(jnp.int32, (1, count * TILE), 1)
        labels = jnp.zeros_like(lane)
        for t in range(count):
            labels = jnp.where(lane >= t * TILE, ref[base + t], labels)
        return labels

    count_ones = []
    for g in range(groups):
        ones = jnp.int32(0)
        for t in range(tiles):
            ones = ones + cd_ref[g * tiles + t]
        count_ones.append(ones)

    def places(j, way):
        lane = lax.broadcasted_iota(jnp.int32, (1, width), 1)
        offsets = [jnp.int32(0), jnp.int32(0)]
        for g in range(groups):
            counted = jnp.logical_and(g >= way, g < j)
            for label, count in ((0, tiles - count_ones[g]), (1, count_ones[g])):
                offsets[label] += jnp.where(counted, jnp.maximum(count - BASE, 0), 0)
        place = jnp.zeros_like(lane)
        pool_place = jnp.zeros_like(lane)
        ones = jnp.int32(0)
        for t in range(tiles):
            label = cd_ref[j * tiles + t]
            rank = jnp.where(label == 1, ones, t - ones)
            left_over = rank - BASE + jnp.where(label == 1, offsets[1], offsets[0])
            left_over = jnp.where(rank >= BASE, left_over, -tiles)
            place = jnp.where(lane >= t * TILE, lane + (rank - t) * TILE, place)
            pool_place = jnp.where(lane >= t * TILE, lane + (left_over - t) * TILE, pool_place)
            ones = ones + label
        return place, pool_place

    def fill(target, place):
        slot = lax.broadcasted_iota(jnp.int32, target.shape, 0)
        target[...] = jnp.where(slot == place, 1.0, 0.0).astype(jnp.bfloat16)

    for t in range(rows // TILE):
        pair_col[pl.ds(t * TILE, TILE), :] = jnp.full((TILE, 1), pair_ref[t], jnp.int32)
    fill(select, places(z, 0)[0])
    own_labels = lane_labels(cd_ref, z * tiles, tiles)

    @pl.loop(0, rows // BLOCK)
    def _(i):
        span = pl.ds(pl.multiple_of(i * BLOCK, BLOCK), BLOCK)
        kept = jnp.where(pair_col[span, :] == own_labels, amp_ref[span, :].astype(jnp.float32), 0.0)
        masked[span, :] = kept.astype(jnp.bfloat16)

    for h in range(HALVES):
        @pl.loop(0, rows // BLOCK)
        def _(i, h=h):
            span = pl.ds(pl.multiple_of(i * BLOCK, BLOCK), BLOCK)
            tile = lax.dot_general(
                select[pl.ds(h * half, half), :], masked[span, :],
                (((1,), (1,)), ((), ())), preferred_element_type=jnp.float32,
            )
            slabs[z, pl.ds(h * half, half), span] = tile.astype(jnp.bfloat16)

        @pl.when(z > 0)
        def _(h=h):
            send_amp(z, h, h, z - 1).start()

        @pl.when(z < last)
        def _(h=h):
            send_amp(z, h, 2 + h, z + 1).start()

    for w in range(groups):
        to_sib(w, 4).start()
    prior.start()

    def send_pool(way):
        return pltpu.make_async_remote_copy(
            src_ref=pool_out.at[way],
            dst_ref=pool_in.at[way],
            send_sem=pool_send.at[way],
            recv_sem=pool_recv.at[way],
            device_id={"col": z + 1 - 2 * way},
            device_id_type=MESH,
        )

    @pl.loop(0, 2)
    def _(way):
        fill(pool_select, places(z, way)[1])

        @pl.loop(0, rows // BLOCK)
        def _(i):
            span = pl.ds(pl.multiple_of(i * BLOCK, BLOCK), BLOCK)
            pool_out[way, :, span] = lax.dot_general(
                pool_select[...], masked[span, :],
                (((1,), (1,)), ((), ())), preferred_element_type=jnp.float32,
            ).astype(jnp.bfloat16)

    @pl.when(z == 0)
    def _():
        send_pool(0).start()
        pool_in[0] = jnp.zeros_like(pool_in[0])

    @pl.when(z == last)
    def _():
        send_pool(1).start()
        pool_in[1] = jnp.zeros_like(pool_in[1])

    def pass_pool(way):
        send_pool(way).wait_recv()
        pool_out[way] = pool_out[way] + pool_in[way]
        send_pool(way).start()

    pool_int[...] = jnp.zeros_like(pool_int)
    for g in range(groups):
        for t in range(tiles):
            cd_col[g, pl.ds(t * TILE, TILE), :] = jnp.full((TILE, 1), cd_ref[g * tiles + t], jnp.int32)
    ab_lane[...] = lane_labels(ab_ref, 0, columns // TILE)

    def pass_on(j, h, send_at, to):
        copy = send_amp(j, h, send_at, to)
        copy.wait_recv()
        copy.start()

    def pass_near(h):
        @pl.when(is_mid)
        def _():
            pass_on(z - 1, h, 4 + h, z + 1)
            pass_on(z + 1, h, 6 + h, z - 1)

    def pass_far(h):
        @pl.when(is_mid)
        def _():
            pass_on(far, h, 8 + h, far_to)

    def take_wave(w):
        recv_int(w, 0)
        fwd_y(w).start()
        recv_int(w, 1)
        fwd_x(w).start()

        @pl.when(w + 2 < groups)
        def _():
            own_x(w + 2).start()
            own_y(w + 2).start()

        to_sib(w, 5).start()
        to_sib(w, 6).start()

    def take_diag(w):
        recv_int(w, 2)
        recv_int(w, 3)
        to_sib(w, 7).start()

    def pair_up(w):
        j = order(w)
        way = (j > z).astype(jnp.int32)
        place, pool_place = places(j, way)
        fill(select, place)
        fill(pool_select, pool_place)

        @pl.loop(0, columns // cols)
        def _(c):
            at = pl.ds(pl.multiple_of(c * cols, cols), cols)
            part = jnp.where(cd_col[j] == ab_lane[:, at], panel[j, :, at].astype(jnp.float32), 0.0)
            part = part.astype(jnp.bfloat16)
            paired_int[:, at] = jnp.dot(
                select[...], part, preferred_element_type=jnp.float32
            ).astype(jnp.bfloat16)
            extra = jnp.dot(pool_select[...], part, preferred_element_type=jnp.float32)
            pool_int[way, :, at] = pool_int[way, :, at] + extra.astype(jnp.bfloat16)

    def wait_amp(w, h):
        @pl.when(jnp.logical_not(is_mid))
        def _():
            send_amp(order(w), h, 0, 0).wait_recv()

    def multiply(left_of, right, store):
        @pl.loop(0, rows // BLOCK)
        def _(i):
            span = pl.ds(pl.multiple_of(i * BLOCK, BLOCK), BLOCK)
            left = left_of(span)

            @pl.loop(0, columns // cols)
            def _(c):
                at = pl.ds(pl.multiple_of(c * cols, cols), cols)
                store(span, at, jnp.dot(left, right[:, at], preferred_element_type=jnp.float32))

    def put(span, at, value):
        total[span, at] = value

    def multiply_slab(w):
        multiply(lambda span: slabs[order(w), :, span].T, paired_int, add)

    def add(span, at, value):
        total[span, at] += value

    def finish(span, at, value):
        ladder = jnp.where(pair_col[span, :] == ab_lane[:, at], total[span, at] + value, 0.0)
        out_ref[span, at] = (res_v[span, at].astype(jnp.float32) + ladder).astype(jnp.bfloat16)

    pass_near(0)
    take_wave(0)
    pass_near(1)
    keep.wait()

    @pl.loop(0, groups - 1)
    def _(w):
        @pl.when(w > 0)
        def _():
            pass_far(w - 1)

        @pl.when(jnp.logical_and(w == 2, is_mid))
        def _():
            pass_pool(z - 1)

        take_wave(w + 1)
        take_diag(w)
        for kind in (4, 5, 6, 7):
            recv_int(w, kind)

        @pl.when(w == 0)
        def _():
            multiply(lambda span: masked[span, :], panel.at[z], put)

        @pl.when(w > 0)
        def _():
            pair_up(w)
            for h in range(HALVES):
                wait_amp(w, h)
            multiply_slab(w)

    take_diag(last)

    @pl.when(is_mid)
    def _():
        pass_pool(2 - z)

    for kind in (4, 5, 6, 7):
        recv_int(last, kind)
    pair_up(last)
    for h in range(HALVES):
        wait_amp(last, h)
    multiply_slab(last)
    prior.wait()

    @pl.when(jnp.logical_not(is_mid))
    def _():
        send_pool((z == 0).astype(jnp.int32)).wait_recv()

    multiply(
        lambda span: pool_in[:, :, span].reshape(2 * pooled, BLOCK).T,
        pool_int.reshape(2 * pooled, columns),
        finish,
    )

    for w in range(groups):
        for copy in (own_x, own_y, fwd_y, fwd_x):
            copy(w).wait_send()
        for kind in (4, 5, 6, 7):
            to_sib(w, kind).wait_send()
    for h in range(HALVES):
        @pl.when(z > 0)
        def _(h=h):
            send_amp(z, h, h, z - 1).wait_send()

        @pl.when(z < last)
        def _(h=h):
            send_amp(z, h, 2 + h, z + 1).wait_send()

        @pl.when(is_mid)
        def _(h=h):
            send_amp(z - 1, h, 4 + h, z + 1).wait_send()
            send_amp(z + 1, h, 6 + h, z - 1).wait_send()
            send_amp(far, h, 8 + h, far_to).wait_send()

    @pl.when(z < last)
    def _():
        send_pool(0).wait_send()

    @pl.when(z > 0)
    def _():
        send_pool(1).wait_send()


def call(slots, ident, pair_class, cd_class, ab_class, amplitudes, integrals, residual_in):
    rows, width = amplitudes.shape
    groups, _, columns = integrals.shape
    smem = pl.BlockSpec(memory_space=pltpu.SMEM)
    vmem = pl.BlockSpec(memory_space=pltpu.VMEM)
    hbm = pl.BlockSpec(memory_space=pl.ANY)
    packed = BASE * TILE
    pooled = slots * TILE
    return pl.pallas_call(
        kernel,
        out_shape=jax.ShapeDtypeStruct((rows, columns), jnp.bfloat16),
        in_specs=[smem] * 3 + [vmem] + [hbm] * 2,
        out_specs=vmem,
        scratch_shapes=[
            pltpu.VMEM((groups, packed, rows), jnp.bfloat16),
            pltpu.VMEM((2, pooled, rows), jnp.bfloat16),
            pltpu.VMEM((2, pooled, rows), jnp.bfloat16),
            pltpu.VMEM((2, pooled, columns), jnp.bfloat16),
            pltpu.VMEM((pooled, width), jnp.bfloat16),
            pltpu.VMEM((groups, width, columns), jnp.bfloat16),
            pltpu.VMEM((packed, columns), jnp.bfloat16),
            pltpu.VMEM((packed, width), jnp.bfloat16),
            pltpu.VMEM((rows, width), jnp.bfloat16),
            pltpu.VMEM((rows, columns), jnp.float32),
            pltpu.VMEM((rows, columns), jnp.bfloat16),
            pltpu.VMEM((rows, 1), jnp.int32),
            pltpu.VMEM((groups, width, 1), jnp.int32),
            pltpu.VMEM((1, columns), jnp.int32),
            pltpu.SemaphoreType.DMA((2,)),
            pltpu.SemaphoreType.DMA((8, groups)),
            pltpu.SemaphoreType.DMA((8, groups)),
            pltpu.SemaphoreType.DMA((10,)),
            pltpu.SemaphoreType.DMA((groups, HALVES)),
            pltpu.SemaphoreType.DMA((2,)),
            pltpu.SemaphoreType.DMA((2,)),
        ],
        compiler_params=pltpu.CompilerParams(
            collective_id=ident, has_side_effects=True, vmem_limit_bytes=56 * 1024 * 1024,
        ),
        cost_estimate=pl.CostEstimate(
            flops=2 * rows * width * groups * columns, bytes_accessed=2 * rows * columns * 3, transcendentals=0,
        ),
        name=f"ladder_{slots}",
    )(pair_class, cd_class, ab_class, amplitudes, integrals, residual_in)


def paired(amplitudes, integrals, residual_in, pair_class, cd_class, ab_class):
    groups = integrals.shape[0]
    per_group = amplitudes.shape[1] // TILE
    ones = jnp.sum(cd_class.reshape(groups, per_group), axis=1)
    left_over = jnp.maximum(jnp.stack([ones, per_group - ones]) - BASE, 0)
    slots = jnp.max(jnp.sum(left_over, axis=1) - jnp.minimum(left_over[:, 0], left_over[:, -1]))
    sizes = (2, 3, 5, (groups - 1) * (per_group - BASE))
    branches = [functools.partial(call, size, ident) for ident, size in enumerate(sizes)]
    which = sum((slots > size).astype(jnp.int32) for size in sizes[:-1])
    return lax.switch(which, branches, pair_class, cd_class, ab_class, amplitudes, integrals, residual_in)


def from_behind(value, axis, steps):
    count = lax.axis_size(axis)
    pairs = [(source, (source + steps) % count) for source in range(count)]
    return lax.ppermute(value, axis, pairs)


def ringed(amplitudes, integrals, residual_in, pair_class, cd_class, ab_class):
    pair_labels = jnp.repeat(pair_class, TILE)
    cd_labels = jnp.repeat(cd_class, TILE)
    ab_labels = jnp.repeat(ab_class, TILE)
    nothing = jnp.zeros((), jnp.bfloat16)
    slab_width = amplitudes.shape[1]

    def mask_amp(values, offset):
        labels = lax.dynamic_slice_in_dim(cd_labels, offset, values.shape[1])
        return jnp.where(pair_labels[:, None] == labels[None, :], values, nothing)

    def mask_int(values, offset):
        labels = lax.dynamic_slice_in_dim(cd_labels, offset, values.shape[0])
        return jnp.where(labels[:, None] == ab_labels[None, :], values, nothing)

    initial = residual_in.astype(jnp.float32)
    col_count = lax.axis_size("col")
    col_index = lax.axis_index("col")

    def contribute(ladder_sum, amp_slab, group_id):
        own_part = lax.dynamic_index_in_dim(integrals, group_id, 0, keepdims=False)
        int_panel = lax.all_gather(own_part, "row", axis=0, tiled=True)
        offset = group_id * slab_width
        return ladder_sum + jnp.dot(
            mask_amp(amp_slab, offset),
            mask_int(int_panel, offset),
            preferred_element_type=jnp.float32,
        )

    ladder_sum = contribute(initial, amplitudes, col_index)

    def advance(counter, state_pair):
        running, amp_slab = state_pair
        amp_slab = from_behind(amp_slab, "col", 1)
        group_id = (col_index - counter) % col_count
        return (contribute(running, amp_slab, group_id), amp_slab)

    ladder_sum, _ = lax.fori_loop(1, col_count, advance, (ladder_sum, amplitudes))
    return ladder_sum.astype(jnp.bfloat16)


def solution(mesh):
    local = paired if (mesh.shape["row"], mesh.shape["col"]) == (8, 4) else ringed
    return jax.shard_map(
        local,
        mesh=mesh,
        in_specs=(P("row", "col"), P(None, "row", "col"), P("row", "col"), P("row"), P(), P("col")),
        out_specs=P("row", "col"),
        check_vma=False,
    )
```

```python
import functools

import jax
import jax.numpy as jnp
from jax import lax
from jax.experimental import pallas as pl
from jax.experimental.pallas import tpu as pltpu
from jax.sharding import PartitionSpec as P

TILE = 96
HALVES = 2
BASE = 4
BLOCK = 256
COLS = 512
MESH = pl.DeviceIdType.MESH


def kernel(pair_ref, cd_ref, ab_ref, amp_ref, int_ref, res_ref, out_ref,
           slabs, pool_in, pool_out, pool_int, pool_select, panel, paired_int, select, masked, total, res_v, pair_col, cd_col, ab_lane,
           local_sem, int_send, int_recv, amp_send, amp_recv, pool_send, pool_recv):
    r = lax.axis_index("row")
    z = lax.axis_index("col")
    last = 3
    core, x, y = lax.rem(r, 2), lax.rem(r // 2, 2), r // 4
    x_nbr, y_nbr, sib = r + 2 - 4 * x, r + 4 - 8 * y, r + 1 - 2 * core
    diag = y_nbr + 2 - 4 * x
    is_mid = jnp.logical_and(z > 0, z < last)
    far = jnp.where(z == 1, 3, 0)
    far_to = jnp.where(z == 1, 0, 3)
    groups, width, columns = panel.shape
    tiles = width // TILE
    rows = amp_ref.shape[0]
    packed = slabs.shape[1]
    half = packed // HALVES
    pooled = pool_in.shape[1]
    cols = COLS if pooled <= COLS else COLS // 2
    def order(w):
        near = jnp.where(w == 1, z - 1, jnp.where(w == 2, z + 1, far))
        there = jnp.where(z == 0, w, jnp.where(z == last, last - w, near))
        return jnp.where(w == 0, z, there)

    barrier = pltpu.get_barrier_semaphore()
    for neighbour in (x_nbr, y_nbr, sib):
        pl.semaphore_signal(barrier, inc=1, device_id={"row": neighbour}, device_id_type=MESH)

    @pl.when(z > 0)
    def _():
        pl.semaphore_signal(barrier, inc=1, device_id={"col": z - 1}, device_id_type=MESH)

    @pl.when(z < last)
    def _():
        pl.semaphore_signal(barrier, inc=1, device_id={"col": z + 1}, device_id_type=MESH)

    def rows_of(owner):
        return pl.ds(pl.multiple_of(owner * TILE, TILE), TILE)

    def send_int(owner, wave, kind, to, own=False, side=None):
        g = order(wave)
        if side is None:
            there = panel.at[g, rows_of(owner), :]
        else:
            there = panel.at[g, rows_of(owner), pl.ds(side * (columns // 2), columns // 2)]
        return pltpu.make_async_remote_copy(
            src_ref=int_ref.at[g] if own else there,
            dst_ref=there,
            send_sem=int_send.at[kind, wave],
            recv_sem=int_recv.at[kind, wave],
            device_id={"row": to},
            device_id_type=MESH,
        )

    def own_x(w):
        return send_int(r, w, 0, x_nbr, own=True)

    def own_y(w):
        return send_int(r, w, 1, y_nbr, own=True)

    def fwd_y(w):
        return send_int(x_nbr, w, 2, y_nbr, side=0)

    def fwd_x(w):
        return send_int(y_nbr, w, 3, x_nbr, side=1)

    def to_sib(w, kind):
        return send_int((r, x_nbr, y_nbr, diag)[kind - 4], w, kind, sib, own=kind == 4)

    def recv_int(w, kind):
        owner = (x_nbr, y_nbr, diag, diag, sib, sib + 2 - 4 * x, sib + 4 - 8 * y, sib + 2 - 4 * x + 4 - 8 * y)[kind]
        send_int(owner, w, kind, sib, side={2: 0, 3: 1}.get(kind)).wait_recv()

    def slab(j, h):
        return slabs.at[j, pl.ds(pl.multiple_of(h * half, 16), half), :]

    def send_amp(j, h, send_at, to):
        return pltpu.make_async_remote_copy(
            src_ref=slab(j, h),
            dst_ref=slab(j, h),
            send_sem=amp_send.at[send_at],
            recv_sem=amp_recv.at[j, h],
            device_id={"col": to},
            device_id_type=MESH,
        )

    keep = pltpu.make_async_copy(int_ref, panel.at[:, rows_of(r), :], local_sem.at[0])
    prior = pltpu.make_async_copy(res_ref, res_v, local_sem.at[1])

    pl.semaphore_wait(barrier, 3 + (z > 0).astype(jnp.int32) + (z < last).astype(jnp.int32))

    for w in (0, 1):
        own_x(w).start()
        own_y(w).start()
    keep.start()

    def lane_labels(ref, base, count):
        lane = lax.broadcasted_iota(jnp.int32, (1, count * TILE), 1)
        labels = jnp.zeros_like(lane)
        for t in range(count):
            labels = jnp.where(lane >= t * TILE, ref[base + t], labels)
        return labels

    count_ones = []
    for g in range(groups):
        ones = jnp.int32(0)
        for t in range(tiles):
            ones = ones + cd_ref[g * tiles + t]
        count_ones.append(ones)

    def places(j, way):
        lane = lax.broadcasted_iota(jnp.int32, (1, width), 1)
        offsets = [jnp.int32(0), jnp.int32(0)]
        for g in range(groups):
            counted = jnp.logical_and(g >= way, g < j)
            for label, count in ((0, tiles - count_ones[g]), (1, count_ones[g])):
                offsets[label] += jnp.where(counted, jnp.maximum(count - BASE, 0), 0)
        place = jnp.zeros_like(lane)
        pool_place = jnp.zeros_like(lane)
        ones = jnp.int32(0)
        for t in range(tiles):
            label = cd_ref[j * tiles + t]
            rank = jnp.where(label == 1, ones, t - ones)
            left_over = rank - BASE + jnp.where(label == 1, offsets[1], offsets[0])
            left_over = jnp.where(rank >= BASE, left_over, -tiles)
            place = jnp.where(lane >= t * TILE, lane + (rank - t) * TILE, place)
            pool_place = jnp.where(lane >= t * TILE, lane + (left_over - t) * TILE, pool_place)
            ones = ones + label
        return place, pool_place

    def fill(target, place):
        slot = lax.broadcasted_iota(jnp.int32, target.shape, 0)
        target[...] = jnp.where(slot == place, 1.0, 0.0).astype(jnp.bfloat16)

    for t in range(rows // TILE):
        pair_col[pl.ds(t * TILE, TILE), :] = jnp.full((TILE, 1), pair_ref[t], jnp.int32)
    fill(select, places(z, 0)[0])
    own_labels = lane_labels(cd_ref, z * tiles, tiles)

    @pl.loop(0, rows // BLOCK)
    def _(i):
        span = pl.ds(pl.multiple_of(i * BLOCK, BLOCK), BLOCK)
        kept = jnp.where(pair_col[span, :] == own_labels, amp_ref[span, :].astype(jnp.float32), 0.0)
        masked[span, :] = kept.astype(jnp.bfloat16)

    for h in range(HALVES):
        @pl.loop(0, rows // BLOCK)
        def _(i, h=h):
            span = pl.ds(pl.multiple_of(i * BLOCK, BLOCK), BLOCK)
            tile = lax.dot_general(
                select[pl.ds(h * half, half), :], masked[span, :],
                (((1,), (1,)), ((), ())), preferred_element_type=jnp.float32,
            )
            slabs[z, pl.ds(h * half, half), span] = tile.astype(jnp.bfloat16)

        @pl.when(z > 0)
        def _(h=h):
            send_amp(z, h, h, z - 1).start()

        @pl.when(z < last)
        def _(h=h):
            send_amp(z, h, 2 + h, z + 1).start()

    for w in range(groups):
        to_sib(w, 4).start()
    prior.start()

    def send_pool(way):
        return pltpu.make_async_remote_copy(
            src_ref=pool_out.at[way],
            dst_ref=pool_in.at[way],
            send_sem=pool_send.at[way],
            recv_sem=pool_recv.at[way],
            device_id={"col": z + 1 - 2 * way},
            device_id_type=MESH,
        )

    @pl.loop(0, 2)
    def _(way):
        fill(pool_select, places(z, way)[1])

        @pl.loop(0, rows // BLOCK)
        def _(i):
            span = pl.ds(pl.multiple_of(i * BLOCK, BLOCK), BLOCK)
            pool_out[way, :, span] = lax.dot_general(
                pool_select[...], masked[span, :],
                (((1,), (1,)), ((), ())), preferred_element_type=jnp.float32,
            ).astype(jnp.bfloat16)

    @pl.when(z == 0)
    def _():
        send_pool(0).start()

    @pl.when(z == last)
    def _():
        send_pool(1).start()

    def pass_pool(way):
        send_pool(way).wait_recv()
        pool_out[way] = pool_out[way] + pool_in[way]
        send_pool(way).start()

    pool_int[...] = jnp.zeros_like(pool_int)
    for g in range(groups):
        for t in range(tiles):
            cd_col[g, pl.ds(t * TILE, TILE), :] = jnp.full((TILE, 1), cd_ref[g * tiles + t], jnp.int32)
    ab_lane[...] = lane_labels(ab_ref, 0, columns // TILE)

    def pass_on(j, h, send_at, to):
        copy = send_amp(j, h, send_at, to)
        copy.wait_recv()
        copy.start()

    def pass_near(h):
        @pl.when(is_mid)
        def _():
            pass_on(z - 1, h, 4 + h, z + 1)
            pass_on(z + 1, h, 6 + h, z - 1)

    def pass_far(h):
        @pl.when(is_mid)
        def _():
            pass_on(far, h, 8 + h, far_to)

    def take_wave(w):
        recv_int(w, 0)
        fwd_y(w).start()
        recv_int(w, 1)
        fwd_x(w).start()

        @pl.when(w + 2 < groups)
        def _():
            own_x(w + 2).start()
            own_y(w + 2).start()

        to_sib(w, 5).start()
        to_sib(w, 6).start()

    def take_diag(w):
        recv_int(w, 2)
        recv_int(w, 3)
        to_sib(w, 7).start()

    def pair_up(w):
        j = order(w)
        way = (j > z).astype(jnp.int32)
        place, pool_place = places(j, way)
        fill(select, place)
        fill(pool_select, pool_place)

        @pl.loop(0, columns // cols)
        def _(c):
            at = pl.ds(pl.multiple_of(c * cols, cols), cols)
            part = jnp.where(cd_col[j] == ab_lane[:, at], panel[j, :, at].astype(jnp.float32), 0.0)
            part = part.astype(jnp.bfloat16)
            paired_int[:, at] = jnp.dot(
                select[...], part, preferred_element_type=jnp.float32
            ).astype(jnp.bfloat16)
            extra = jnp.dot(pool_select[...], part, preferred_element_type=jnp.float32)
            pool_int[way, :, at] = pool_int[way, :, at] + extra.astype(jnp.bfloat16)

    def wait_amp(w, h):
        @pl.when(jnp.logical_not(is_mid))
        def _():
            send_amp(order(w), h, 0, 0).wait_recv()

    def multiply(left_of, right, store):
        @pl.loop(0, rows // BLOCK)
        def _(i):
            span = pl.ds(pl.multiple_of(i * BLOCK, BLOCK), BLOCK)
            left = left_of(span)

            @pl.loop(0, columns // cols)
            def _(c):
                at = pl.ds(pl.multiple_of(c * cols, cols), cols)
                store(span, at, jnp.dot(left, right[:, at], preferred_element_type=jnp.float32))

    def put(span, at, value):
        total[span, at] = value

    def multiply_slab(w):
        multiply(lambda span: slabs[order(w), :, span].T, paired_int, add)

    def add(span, at, value):
        total[span, at] += value

    def finish(span, at, value):
        ladder = jnp.where(pair_col[span, :] == ab_lane[:, at], total[span, at] + value, 0.0)
        out_ref[span, at] = (res_v[span, at].astype(jnp.float32) + ladder).astype(jnp.bfloat16)

    pass_near(0)
    take_wave(0)
    pass_near(1)
    keep.wait()

    last_way = (z < 2).astype(jnp.int32)

    def multiply_pool(way, store):
        multiply(lambda span: pool_in[way, :, span].T, pool_int.at[way], store)

    @pl.loop(0, groups - 1)
    def _(w):
        take_wave(w + 1)

        @pl.when(w == 0)
        def _():
            pass_far(0)

        take_diag(w)
        for kind in (4, 5, 6, 7):
            recv_int(w, kind)

        @pl.when(w == 0)
        def _():
            multiply(lambda span: masked[span, :], panel.at[z], put)
            pass_far(1)

            @pl.when(is_mid)
            def _():
                pass_pool(1 - last_way)

        @pl.when(w > 0)
        def _():
            pair_up(w)
            for h in range(HALVES):
                wait_amp(w, h)
            multiply_slab(w)

        @pl.when(jnp.logical_and(w == 1, is_mid))
        def _():
            pass_pool(last_way)

    take_diag(last)
    for kind in (4, 5, 6, 7):
        recv_int(last, kind)
    pair_up(last)

    @pl.when(is_mid)
    def _():
        multiply_pool(1 - last_way, add)

    for h in range(HALVES):
        wait_amp(last, h)
    multiply_slab(last)
    prior.wait()

    @pl.when(jnp.logical_not(is_mid))
    def _():
        send_pool(last_way).wait_recv()

    multiply_pool(last_way, finish)

    for w in range(groups):
        for copy in (own_x, own_y, fwd_y, fwd_x):
            copy(w).wait_send()
        for kind in (4, 5, 6, 7):
            to_sib(w, kind).wait_send()
    for h in range(HALVES):
        @pl.when(z > 0)
        def _(h=h):
            send_amp(z, h, h, z - 1).wait_send()

        @pl.when(z < last)
        def _(h=h):
            send_amp(z, h, 2 + h, z + 1).wait_send()

        @pl.when(is_mid)
        def _(h=h):
            send_amp(z - 1, h, 4 + h, z + 1).wait_send()
            send_amp(z + 1, h, 6 + h, z - 1).wait_send()
            send_amp(far, h, 8 + h, far_to).wait_send()

    @pl.when(z < last)
    def _():
        send_pool(0).wait_send()

    @pl.when(z > 0)
    def _():
        send_pool(1).wait_send()


def call(slots, ident, pair_class, cd_class, ab_class, amplitudes, integrals, residual_in):
    rows, width = amplitudes.shape
    groups, _, columns = integrals.shape
    smem = pl.BlockSpec(memory_space=pltpu.SMEM)
    vmem = pl.BlockSpec(memory_space=pltpu.VMEM)
    hbm = pl.BlockSpec(memory_space=pl.ANY)
    packed = BASE * TILE
    pooled = slots * TILE
    return pl.pallas_call(
        kernel,
        out_shape=jax.ShapeDtypeStruct((rows, columns), jnp.bfloat16),
        in_specs=[smem] * 3 + [vmem] + [hbm] * 2,
        out_specs=vmem,
        scratch_shapes=[
            pltpu.VMEM((groups, packed, rows), jnp.bfloat16),
            pltpu.VMEM((2, pooled, rows), jnp.bfloat16),
            pltpu.VMEM((2, pooled, rows), jnp.bfloat16),
            pltpu.VMEM((2, pooled, columns), jnp.bfloat16),
            pltpu.VMEM((pooled, width), jnp.bfloat16),
            pltpu.VMEM((groups, width, columns), jnp.bfloat16),
            pltpu.VMEM((packed, columns), jnp.bfloat16),
            pltpu.VMEM((packed, width), jnp.bfloat16),
            pltpu.VMEM((rows, width), jnp.bfloat16),
            pltpu.VMEM((rows, columns), jnp.float32),
            pltpu.VMEM((rows, columns), jnp.bfloat16),
            pltpu.VMEM((rows, 1), jnp.int32),
            pltpu.VMEM((groups, width, 1), jnp.int32),
            pltpu.VMEM((1, columns), jnp.int32),
            pltpu.SemaphoreType.DMA((2,)),
            pltpu.SemaphoreType.DMA((8, groups)),
            pltpu.SemaphoreType.DMA((8, groups)),
            pltpu.SemaphoreType.DMA((10,)),
            pltpu.SemaphoreType.DMA((groups, HALVES)),
            pltpu.SemaphoreType.DMA((2,)),
            pltpu.SemaphoreType.DMA((2,)),
        ],
        compiler_params=pltpu.CompilerParams(
            collective_id=ident, has_side_effects=True, vmem_limit_bytes=56 * 1024 * 1024,
        ),
        cost_estimate=pl.CostEstimate(
            flops=2 * rows * width * groups * columns, bytes_accessed=2 * rows * columns * 3, transcendentals=0,
        ),
        name=f"ladder_{slots}",
    )(pair_class, cd_class, ab_class, amplitudes, integrals, residual_in)


def pool_sizes(groups, per_group):
    return (2, 3, 5, (groups - 1) * (per_group - BASE))


def choose(groups, per_group, cd_ref, which_ref):
    needed = jnp.int32(0)
    for label in (0, 1):
        left_over = []
        for g in range(groups):
            count = jnp.int32(0)
            for t in range(per_group):
                count += (cd_ref[g * per_group + t] == label).astype(jnp.int32)
            left_over.append(jnp.maximum(count - BASE, 0))
        ends = jnp.minimum(left_over[0], left_over[-1])
        needed = jnp.maximum(needed, sum(left_over) - ends)
    sizes = pool_sizes(groups, per_group)
    which_ref[0] = sum((needed > size).astype(jnp.int32) for size in sizes[:-1])


def paired(amplitudes, integrals, residual_in, pair_class, cd_class, ab_class):
    groups = integrals.shape[0]
    per_group = amplitudes.shape[1] // TILE
    smem = pl.BlockSpec(memory_space=pltpu.SMEM)
    which = pl.pallas_call(
        functools.partial(choose, groups, per_group),
        out_shape=jax.ShapeDtypeStruct((1,), jnp.int32),
        in_specs=[smem],
        out_specs=smem,
        name="choose",
    )(cd_class)
    branches = [functools.partial(call, size, ident) for ident, size in enumerate(pool_sizes(groups, per_group))]
    return lax.switch(which[0], branches, pair_class, cd_class, ab_class, amplitudes, integrals, residual_in)


def from_behind(value, axis, steps):
    count = lax.axis_size(axis)
    pairs = [(source, (source + steps) % count) for source in range(count)]
    return lax.ppermute(value, axis, pairs)


def ringed(amplitudes, integrals, residual_in, pair_class, cd_class, ab_class):
    pair_labels = jnp.repeat(pair_class, TILE)
    cd_labels = jnp.repeat(cd_class, TILE)
    ab_labels = jnp.repeat(ab_class, TILE)
    nothing = jnp.zeros((), jnp.bfloat16)
    slab_width = amplitudes.shape[1]

    def mask_amp(values, offset):
        labels = lax.dynamic_slice_in_dim(cd_labels, offset, values.shape[1])
        return jnp.where(pair_labels[:, None] == labels[None, :], values, nothing)

    def mask_int(values, offset):
        labels = lax.dynamic_slice_in_dim(cd_labels, offset, values.shape[0])
        return jnp.where(labels[:, None] == ab_labels[None, :], values, nothing)

    initial = residual_in.astype(jnp.float32)
    col_count = lax.axis_size("col")
    col_index = lax.axis_index("col")

    def contribute(ladder_sum, amp_slab, group_id):
        own_part = lax.dynamic_index_in_dim(integrals, group_id, 0, keepdims=False)
        int_panel = lax.all_gather(own_part, "row", axis=0, tiled=True)
        offset = group_id * slab_width
        return ladder_sum + jnp.dot(
            mask_amp(amp_slab, offset),
            mask_int(int_panel, offset),
            preferred_element_type=jnp.float32,
        )

    ladder_sum = contribute(initial, amplitudes, col_index)

    def advance(counter, state_pair):
        running, amp_slab = state_pair
        amp_slab = from_behind(amp_slab, "col", 1)
        group_id = (col_index - counter) % col_count
        return (contribute(running, amp_slab, group_id), amp_slab)

    ladder_sum, _ = lax.fori_loop(1, col_count, advance, (ladder_sum, amplitudes))
    return ladder_sum.astype(jnp.bfloat16)


def solution(mesh):
    local = paired if (mesh.shape["row"], mesh.shape["col"]) == (8, 4) else ringed
    return jax.shard_map(
        local,
        mesh=mesh,
        in_specs=(P("row", "col"), P(None, "row", "col"), P("row", "col"), P("row"), P(), P("col")),
        out_specs=P("row", "col"),
        check_vma=False,
    )
```

```python
import functools

import jax
import jax.numpy as jnp
from jax import lax
from jax.experimental import pallas as pl
from jax.experimental.pallas import tpu as pltpu
from jax.sharding import PartitionSpec as P

TILE = 96
HALVES = 2
BASE = 4
BLOCK = 256
COLS = 512
MESH = pl.DeviceIdType.MESH


def kernel(pair_ref, cd_ref, ab_ref, amp_ref, int_ref, res_ref, out_ref,
           slabs, pool_in, pool_out, pool_int, pool_select, panel, paired_int, select, masked, total, res_v, pair_col, cd_col, ab_lane,
           local_sem, int_send, int_recv, amp_send, amp_recv, pool_send, pool_recv):
    r = lax.axis_index("row")
    z = lax.axis_index("col")
    last = 3
    core, x, y = lax.rem(r, 2), lax.rem(r // 2, 2), r // 4
    x_nbr, y_nbr, sib = r + 2 - 4 * x, r + 4 - 8 * y, r + 1 - 2 * core
    diag = y_nbr + 2 - 4 * x
    is_mid = jnp.logical_and(z > 0, z < last)
    far = jnp.where(z == 1, 3, 0)
    far_to = jnp.where(z == 1, 0, 3)
    groups, width, columns = panel.shape
    tiles = width // TILE
    rows = amp_ref.shape[0]
    packed = slabs.shape[1]
    half = packed // HALVES
    pooled = pool_in.shape[1]
    cols = COLS if pooled <= COLS else COLS // 2
    def order(w):
        near = jnp.where(w == 1, z - 1, jnp.where(w == 2, z + 1, far))
        there = jnp.where(z == 0, w, jnp.where(z == last, last - w, near))
        return jnp.where(w == 0, z, there)

    barrier = pltpu.get_barrier_semaphore()
    for neighbour in (x_nbr, y_nbr, sib):
        pl.semaphore_signal(barrier, inc=1, device_id={"row": neighbour}, device_id_type=MESH)

    @pl.when(z > 0)
    def _():
        pl.semaphore_signal(barrier, inc=1, device_id={"col": z - 1}, device_id_type=MESH)

    @pl.when(z < last)
    def _():
        pl.semaphore_signal(barrier, inc=1, device_id={"col": z + 1}, device_id_type=MESH)

    def rows_of(owner):
        return pl.ds(pl.multiple_of(owner * TILE, TILE), TILE)

    def send_int(owner, wave, kind, to, own=False, side=None):
        g = order(wave)
        if side is None:
            there = panel.at[g, rows_of(owner), :]
        else:
            there = panel.at[g, rows_of(owner), pl.ds(side * (columns // 2), columns // 2)]
        return pltpu.make_async_remote_copy(
            src_ref=int_ref.at[g] if own else there,
            dst_ref=there,
            send_sem=int_send.at[kind, wave],
            recv_sem=int_recv.at[kind, wave],
            device_id={"row": to},
            device_id_type=MESH,
        )

    def own_x(w):
        return send_int(r, w, 0, x_nbr, own=True)

    def own_y(w):
        return send_int(r, w, 1, y_nbr, own=True)

    def fwd_y(w):
        return send_int(x_nbr, w, 2, y_nbr, side=0)

    def fwd_x(w):
        return send_int(y_nbr, w, 3, x_nbr, side=1)

    def to_sib(w, kind):
        return send_int((r, x_nbr, y_nbr, diag)[kind - 4], w, kind, sib, own=kind == 4)

    def recv_int(w, kind):
        owner = (x_nbr, y_nbr, diag, diag, sib, sib + 2 - 4 * x, sib + 4 - 8 * y, sib + 2 - 4 * x + 4 - 8 * y)[kind]
        send_int(owner, w, kind, sib, side={2: 0, 3: 1}.get(kind)).wait_recv()

    def slab(j, h):
        return slabs.at[j, pl.ds(pl.multiple_of(h * half, 16), half), :]

    def send_amp(j, h, send_at, to):
        return pltpu.make_async_remote_copy(
            src_ref=slab(j, h),
            dst_ref=slab(j, h),
            send_sem=amp_send.at[send_at],
            recv_sem=amp_recv.at[j, h],
            device_id={"col": to},
            device_id_type=MESH,
        )

    keep = pltpu.make_async_copy(int_ref, panel.at[:, rows_of(r), :], local_sem.at[0])
    prior = pltpu.make_async_copy(res_ref, res_v, local_sem.at[1])

    pl.semaphore_wait(barrier, 3 + (z > 0).astype(jnp.int32) + (z < last).astype(jnp.int32))

    for w in (0, 1):
        own_x(w).start()
        own_y(w).start()
    keep.start()

    def lane_labels(ref, base, count):
        lane = lax.broadcasted_iota(jnp.int32, (1, count * TILE), 1)
        labels = jnp.zeros_like(lane)
        for t in range(count):
            labels = jnp.where(lane >= t * TILE, ref[base + t], labels)
        return labels

    count_ones = []
    for g in range(groups):
        ones = jnp.int32(0)
        for t in range(tiles):
            ones = ones + cd_ref[g * tiles + t]
        count_ones.append(ones)

    def places(j, way):
        lane = lax.broadcasted_iota(jnp.int32, (1, width), 1)
        offsets = [jnp.int32(0), jnp.int32(0)]
        for g in range(groups):
            counted = jnp.logical_and(g >= way, g < j)
            for label, count in ((0, tiles - count_ones[g]), (1, count_ones[g])):
                offsets[label] += jnp.where(counted, jnp.maximum(count - BASE, 0), 0)
        place = jnp.zeros_like(lane)
        pool_place = jnp.zeros_like(lane)
        ones = jnp.int32(0)
        for t in range(tiles):
            label = cd_ref[j * tiles + t]
            rank = jnp.where(label == 1, ones, t - ones)
            left_over = rank - BASE + jnp.where(label == 1, offsets[1], offsets[0])
            left_over = jnp.where(rank >= BASE, left_over, -tiles)
            place = jnp.where(lane >= t * TILE, lane + (rank - t) * TILE, place)
            pool_place = jnp.where(lane >= t * TILE, lane + (left_over - t) * TILE, pool_place)
            ones = ones + label
        return place, pool_place

    def fill(target, place):
        slot = lax.broadcasted_iota(jnp.int32, target.shape, 0)
        target[...] = jnp.where(slot == place, 1.0, 0.0).astype(jnp.bfloat16)

    for t in range(rows // TILE):
        pair_col[pl.ds(t * TILE, TILE), :] = jnp.full((TILE, 1), pair_ref[t], jnp.int32)
    fill(select, places(z, 0)[0])
    own_labels = lane_labels(cd_ref, z * tiles, tiles)

    @pl.loop(0, rows // BLOCK)
    def _(i):
        span = pl.ds(pl.multiple_of(i * BLOCK, BLOCK), BLOCK)
        kept = jnp.where(pair_col[span, :] == own_labels, amp_ref[span, :].astype(jnp.float32), 0.0)
        masked[span, :] = kept.astype(jnp.bfloat16)

    for h in range(HALVES):
        @pl.loop(0, rows // BLOCK)
        def _(i, h=h):
            span = pl.ds(pl.multiple_of(i * BLOCK, BLOCK), BLOCK)
            tile = lax.dot_general(
                select[pl.ds(h * half, half), :], masked[span, :],
                (((1,), (1,)), ((), ())), preferred_element_type=jnp.float32,
            )
            slabs[z, pl.ds(h * half, half), span] = tile.astype(jnp.bfloat16)

        @pl.when(z > 0)
        def _(h=h):
            send_amp(z, h, h, z - 1).start()

        @pl.when(z < last)
        def _(h=h):
            send_amp(z, h, 2 + h, z + 1).start()

    for w in range(groups):
        to_sib(w, 4).start()
    prior.start()

    def send_pool(way, h):
        span = pl.ds(h * (pooled // HALVES), pooled // HALVES)
        return pltpu.make_async_remote_copy(
            src_ref=pool_out.at[way, span, :],
            dst_ref=pool_in.at[way, span, :],
            send_sem=pool_send.at[way, h],
            recv_sem=pool_recv.at[way, h],
            device_id={"col": z + 1 - 2 * way},
            device_id_type=MESH,
        )

    @pl.loop(0, 2)
    def _(way):
        fill(pool_select, places(z, way)[1])

        @pl.loop(0, rows // BLOCK)
        def _(i):
            span = pl.ds(pl.multiple_of(i * BLOCK, BLOCK), BLOCK)
            pool_out[way, :, span] = lax.dot_general(
                pool_select[...], masked[span, :],
                (((1,), (1,)), ((), ())), preferred_element_type=jnp.float32,
            ).astype(jnp.bfloat16)

    @pl.when(z == 0)
    def _():
        for h in range(HALVES):
            send_pool(0, h).start()

    @pl.when(z == last)
    def _():
        for h in range(HALVES):
            send_pool(1, h).start()

    def pass_pool(way):
        for h in range(HALVES):
            span = pl.ds(h * (pooled // HALVES), pooled // HALVES)
            send_pool(way, h).wait_recv()
            pool_out[way, span, :] = pool_out[way, span, :] + pool_in[way, span, :]
            send_pool(way, h).start()

    pool_int[...] = jnp.zeros_like(pool_int)
    for g in range(groups):
        for t in range(tiles):
            cd_col[g, pl.ds(t * TILE, TILE), :] = jnp.full((TILE, 1), cd_ref[g * tiles + t], jnp.int32)
    ab_lane[...] = lane_labels(ab_ref, 0, columns // TILE)

    def pass_on(j, h, send_at, to):
        copy = send_amp(j, h, send_at, to)
        copy.wait_recv()
        copy.start()

    def pass_near(h):
        @pl.when(is_mid)
        def _():
            pass_on(z - 1, h, 4 + h, z + 1)
            pass_on(z + 1, h, 6 + h, z - 1)

    def pass_far(h):
        @pl.when(is_mid)
        def _():
            pass_on(far, h, 8 + h, far_to)

    def take_wave(w):
        recv_int(w, 0)
        fwd_y(w).start()
        recv_int(w, 1)
        fwd_x(w).start()

        @pl.when(w + 2 < groups)
        def _():
            own_x(w + 2).start()
            own_y(w + 2).start()

        to_sib(w, 5).start()
        to_sib(w, 6).start()

    def take_diag(w):
        recv_int(w, 2)
        recv_int(w, 3)
        to_sib(w, 7).start()

    def pair_up(w):
        j = order(w)
        way = (j > z).astype(jnp.int32)
        place, pool_place = places(j, way)
        fill(select, place)
        fill(pool_select, pool_place)

        @pl.loop(0, columns // cols)
        def _(c):
            at = pl.ds(pl.multiple_of(c * cols, cols), cols)
            part = jnp.where(cd_col[j] == ab_lane[:, at], panel[j, :, at].astype(jnp.float32), 0.0)
            part = part.astype(jnp.bfloat16)
            paired_int[:, at] = jnp.dot(
                select[...], part, preferred_element_type=jnp.float32
            ).astype(jnp.bfloat16)
            extra = jnp.dot(pool_select[...], part, preferred_element_type=jnp.float32)
            pool_int[way, :, at] = pool_int[way, :, at] + extra.astype(jnp.bfloat16)

    def wait_amp(w, h):
        @pl.when(jnp.logical_not(is_mid))
        def _():
            send_amp(order(w), h, 0, 0).wait_recv()

    def multiply(left_of, right, store):
        @pl.loop(0, rows // BLOCK)
        def _(i):
            span = pl.ds(pl.multiple_of(i * BLOCK, BLOCK), BLOCK)
            left = left_of(span)

            @pl.loop(0, columns // cols)
            def _(c):
                at = pl.ds(pl.multiple_of(c * cols, cols), cols)
                store(span, at, jnp.dot(left, right[:, at], preferred_element_type=jnp.float32))

    def put(span, at, value):
        total[span, at] = value

    def multiply_slab(w):
        multiply(lambda span: slabs[order(w), :, span].T, paired_int, add)

    def add(span, at, value):
        total[span, at] += value

    def finish(span, at, value):
        ladder = jnp.where(pair_col[span, :] == ab_lane[:, at], total[span, at] + value, 0.0)
        out_ref[span, at] = (res_v[span, at].astype(jnp.float32) + ladder).astype(jnp.bfloat16)

    pass_near(0)
    take_wave(0)
    pass_near(1)
    keep.wait()

    last_way = (z < 2).astype(jnp.int32)

    def multiply_pool(way, store):
        multiply(lambda span: pool_in[way, :, span].T, pool_int.at[way], store)

    @pl.loop(0, groups - 1)
    def _(w):
        take_wave(w + 1)

        @pl.when(w == 0)
        def _():
            pass_far(0)

        take_diag(w)
        for kind in (4, 5, 6, 7):
            recv_int(w, kind)

        @pl.when(w == 0)
        def _():
            multiply(lambda span: masked[span, :], panel.at[z], put)
            pass_far(1)

            @pl.when(is_mid)
            def _():
                pass_pool(1 - last_way)

        @pl.when(w > 0)
        def _():
            pair_up(w)

            @pl.when(jnp.logical_and(w == 2, is_mid))
            def _():
                pass_pool(last_way)

            for h in range(HALVES):
                wait_amp(w, h)
            multiply_slab(w)

    take_diag(last)
    for kind in (4, 5, 6, 7):
        recv_int(last, kind)
    pair_up(last)

    @pl.when(is_mid)
    def _():
        multiply_pool(1 - last_way, add)

    for h in range(HALVES):
        wait_amp(last, h)
    multiply_slab(last)
    prior.wait()

    @pl.when(jnp.logical_not(is_mid))
    def _():
        for h in range(HALVES):
            send_pool(last_way, h).wait_recv()

    multiply_pool(last_way, finish)

    for w in range(groups):
        for copy in (own_x, own_y, fwd_y, fwd_x):
            copy(w).wait_send()
        for kind in (4, 5, 6, 7):
            to_sib(w, kind).wait_send()
    for h in range(HALVES):
        @pl.when(z > 0)
        def _(h=h):
            send_amp(z, h, h, z - 1).wait_send()

        @pl.when(z < last)
        def _(h=h):
            send_amp(z, h, 2 + h, z + 1).wait_send()

        @pl.when(is_mid)
        def _(h=h):
            send_amp(z - 1, h, 4 + h, z + 1).wait_send()
            send_amp(z + 1, h, 6 + h, z - 1).wait_send()
            send_amp(far, h, 8 + h, far_to).wait_send()

    @pl.when(z < last)
    def _():
        for h in range(HALVES):
            send_pool(0, h).wait_send()

    @pl.when(z > 0)
    def _():
        for h in range(HALVES):
            send_pool(1, h).wait_send()


def call(slots, ident, pair_class, cd_class, ab_class, amplitudes, integrals, residual_in):
    rows, width = amplitudes.shape
    groups, _, columns = integrals.shape
    smem = pl.BlockSpec(memory_space=pltpu.SMEM)
    vmem = pl.BlockSpec(memory_space=pltpu.VMEM)
    hbm = pl.BlockSpec(memory_space=pl.ANY)
    packed = BASE * TILE
    pooled = slots * TILE
    return pl.pallas_call(
        kernel,
        out_shape=jax.ShapeDtypeStruct((rows, columns), jnp.bfloat16),
        in_specs=[smem] * 3 + [vmem] + [hbm] * 2,
        out_specs=vmem,
        scratch_shapes=[
            pltpu.VMEM((groups, packed, rows), jnp.bfloat16),
            pltpu.VMEM((2, pooled, rows), jnp.bfloat16),
            pltpu.VMEM((2, pooled, rows), jnp.bfloat16),
            pltpu.VMEM((2, pooled, columns), jnp.bfloat16),
            pltpu.VMEM((pooled, width), jnp.bfloat16),
            pltpu.VMEM((groups, width, columns), jnp.bfloat16),
            pltpu.VMEM((packed, columns), jnp.bfloat16),
            pltpu.VMEM((packed, width), jnp.bfloat16),
            pltpu.VMEM((rows, width), jnp.bfloat16),
            pltpu.VMEM((rows, columns), jnp.float32),
            pltpu.VMEM((rows, columns), jnp.bfloat16),
            pltpu.VMEM((rows, 1), jnp.int32),
            pltpu.VMEM((groups, width, 1), jnp.int32),
            pltpu.VMEM((1, columns), jnp.int32),
            pltpu.SemaphoreType.DMA((2,)),
            pltpu.SemaphoreType.DMA((8, groups)),
            pltpu.SemaphoreType.DMA((8, groups)),
            pltpu.SemaphoreType.DMA((10,)),
            pltpu.SemaphoreType.DMA((groups, HALVES)),
            pltpu.SemaphoreType.DMA((2, HALVES)),
            pltpu.SemaphoreType.DMA((2, HALVES)),
        ],
        compiler_params=pltpu.CompilerParams(
            collective_id=ident, has_side_effects=True, vmem_limit_bytes=56 * 1024 * 1024,
        ),
        cost_estimate=pl.CostEstimate(
            flops=2 * rows * width * groups * columns, bytes_accessed=2 * rows * columns * 3, transcendentals=0,
        ),
        name=f"ladder_{slots}",
    )(pair_class, cd_class, ab_class, amplitudes, integrals, residual_in)


def pool_sizes(groups, per_group):
    return (2, 3, 5, (groups - 1) * (per_group - BASE))


def choose(groups, per_group, cd_ref, which_ref):
    needed = jnp.int32(0)
    for label in (0, 1):
        left_over = []
        for g in range(groups):
            count = jnp.int32(0)
            for t in range(per_group):
                count += (cd_ref[g * per_group + t] == label).astype(jnp.int32)
            left_over.append(jnp.maximum(count - BASE, 0))
        ends = jnp.minimum(left_over[0], left_over[-1])
        needed = jnp.maximum(needed, sum(left_over) - ends)
    sizes = pool_sizes(groups, per_group)
    which_ref[0] = sum((needed > size).astype(jnp.int32) for size in sizes[:-1])


def paired(amplitudes, integrals, residual_in, pair_class, cd_class, ab_class):
    groups = integrals.shape[0]
    per_group = amplitudes.shape[1] // TILE
    smem = pl.BlockSpec(memory_space=pltpu.SMEM)
    which = pl.pallas_call(
        functools.partial(choose, groups, per_group),
        out_shape=jax.ShapeDtypeStruct((1,), jnp.int32),
        in_specs=[smem],
        out_specs=smem,
        name="choose",
    )(cd_class)
    branches = [functools.partial(call, size, ident) for ident, size in enumerate(pool_sizes(groups, per_group))]
    return lax.switch(which[0], branches, pair_class, cd_class, ab_class, amplitudes, integrals, residual_in)


def from_behind(value, axis, steps):
    count = lax.axis_size(axis)
    pairs = [(source, (source + steps) % count) for source in range(count)]
    return lax.ppermute(value, axis, pairs)


def ringed(amplitudes, integrals, residual_in, pair_class, cd_class, ab_class):
    pair_labels = jnp.repeat(pair_class, TILE)
    cd_labels = jnp.repeat(cd_class, TILE)
    ab_labels = jnp.repeat(ab_class, TILE)
    nothing = jnp.zeros((), jnp.bfloat16)
    slab_width = amplitudes.shape[1]

    def mask_amp(values, offset):
        labels = lax.dynamic_slice_in_dim(cd_labels, offset, values.shape[1])
        return jnp.where(pair_labels[:, None] == labels[None, :], values, nothing)

    def mask_int(values, offset):
        labels = lax.dynamic_slice_in_dim(cd_labels, offset, values.shape[0])
        return jnp.where(labels[:, None] == ab_labels[None, :], values, nothing)

    initial = residual_in.astype(jnp.float32)
    col_count = lax.axis_size("col")
    col_index = lax.axis_index("col")

    def contribute(ladder_sum, amp_slab, group_id):
        own_part = lax.dynamic_index_in_dim(integrals, group_id, 0, keepdims=False)
        int_panel = lax.all_gather(own_part, "row", axis=0, tiled=True)
        offset = group_id * slab_width
        return ladder_sum + jnp.dot(
            mask_amp(amp_slab, offset),
            mask_int(int_panel, offset),
            preferred_element_type=jnp.float32,
        )

    ladder_sum = contribute(initial, amplitudes, col_index)

    def advance(counter, state_pair):
        running, amp_slab = state_pair
        amp_slab = from_behind(amp_slab, "col", 1)
        group_id = (col_index - counter) % col_count
        return (contribute(running, amp_slab, group_id), amp_slab)

    ladder_sum, _ = lax.fori_loop(1, col_count, advance, (ladder_sum, amplitudes))
    return ladder_sum.astype(jnp.bfloat16)


def solution(mesh):
    local = paired if (mesh.shape["row"], mesh.shape["col"]) == (8, 4) else ringed
    return jax.shard_map(
        local,
        mesh=mesh,
        in_specs=(P("row", "col"), P(None, "row", "col"), P("row", "col"), P("row"), P(), P("col")),
        out_specs=P("row", "col"),
        check_vma=False,
    )
```

```python
import functools

import jax
import jax.numpy as jnp
from jax import lax
from jax.experimental import pallas as pl
from jax.experimental.pallas import tpu as pltpu
from jax.sharding import PartitionSpec as P

TILE = 96
HALVES = 2
BASE = 4
BLOCK = 256
COLS = 512
MESH = pl.DeviceIdType.MESH


def kernel(pair_ref, cd_ref, ab_ref, amp_ref, int_ref, res_ref, out_ref,
           slabs, pool_in, pool_out, pool_int, pool_select, panel, paired_int, select, masked, total, res_v, pair_col, cd_col, ab_lane,
           local_sem, int_send, int_recv, amp_send, amp_recv, pool_send, pool_recv):
    r = lax.axis_index("row")
    z = lax.axis_index("col")
    last = 3
    core, x, y = lax.rem(r, 2), lax.rem(r // 2, 2), r // 4
    x_nbr, y_nbr, sib = r + 2 - 4 * x, r + 4 - 8 * y, r + 1 - 2 * core
    diag = y_nbr + 2 - 4 * x
    is_mid = jnp.logical_and(z > 0, z < last)
    far = jnp.where(z == 1, 3, 0)
    far_to = jnp.where(z == 1, 0, 3)
    groups, width, columns = panel.shape
    tiles = width // TILE
    rows = amp_ref.shape[0]
    packed = slabs.shape[1]
    half = packed // HALVES
    pooled = pool_in.shape[1]
    cols = COLS if pooled <= COLS else COLS // 2
    def order(w):
        near = jnp.where(w == 1, z - 1, jnp.where(w == 2, z + 1, far))
        there = jnp.where(z == 0, w, jnp.where(z == last, last - w, near))
        return jnp.where(w == 0, z, there)

    barrier = pltpu.get_barrier_semaphore()
    for neighbour in (x_nbr, y_nbr, sib):
        pl.semaphore_signal(barrier, inc=1, device_id={"row": neighbour}, device_id_type=MESH)

    @pl.when(z > 0)
    def _():
        pl.semaphore_signal(barrier, inc=1, device_id={"col": z - 1}, device_id_type=MESH)

    @pl.when(z < last)
    def _():
        pl.semaphore_signal(barrier, inc=1, device_id={"col": z + 1}, device_id_type=MESH)

    def rows_of(owner):
        return pl.ds(pl.multiple_of(owner * TILE, TILE), TILE)

    def send_int(owner, wave, kind, to, own=False, side=None):
        g = order(wave)
        if side is None:
            there = panel.at[g, rows_of(owner), :]
        else:
            there = panel.at[g, rows_of(owner), pl.ds(side * (columns // 2), columns // 2)]
        return pltpu.make_async_remote_copy(
            src_ref=int_ref.at[g] if own else there,
            dst_ref=there,
            send_sem=int_send.at[kind, wave],
            recv_sem=int_recv.at[kind, wave],
            device_id={"row": to},
            device_id_type=MESH,
        )

    def own_x(w):
        return send_int(r, w, 0, x_nbr, own=True)

    def own_y(w):
        return send_int(r, w, 1, y_nbr, own=True)

    def fwd_y(w):
        return send_int(x_nbr, w, 2, y_nbr, side=0)

    def fwd_x(w):
        return send_int(y_nbr, w, 3, x_nbr, side=1)

    def to_sib(w, kind):
        return send_int((r, x_nbr, y_nbr, diag)[kind - 4], w, kind, sib, own=kind == 4)

    def recv_int(w, kind):
        owner = (x_nbr, y_nbr, diag, diag, sib, sib + 2 - 4 * x, sib + 4 - 8 * y, sib + 2 - 4 * x + 4 - 8 * y)[kind]
        send_int(owner, w, kind, sib, side={2: 0, 3: 1}.get(kind)).wait_recv()

    def slab(j, h):
        return slabs.at[j, pl.ds(pl.multiple_of(h * half, 16), half), :]

    def send_amp(j, h, send_at, to):
        return pltpu.make_async_remote_copy(
            src_ref=slab(j, h),
            dst_ref=slab(j, h),
            send_sem=amp_send.at[send_at],
            recv_sem=amp_recv.at[j, h],
            device_id={"col": to},
            device_id_type=MESH,
        )

    keep = pltpu.make_async_copy(int_ref, panel.at[:, rows_of(r), :], local_sem.at[0])
    prior = pltpu.make_async_copy(res_ref, res_v, local_sem.at[1])

    pl.semaphore_wait(barrier, 3 + (z > 0).astype(jnp.int32) + (z < last).astype(jnp.int32))

    for w in (0, 1):
        own_x(w).start()
        own_y(w).start()
    keep.start()

    def lane_labels(ref, base, count):
        lane = lax.broadcasted_iota(jnp.int32, (1, count * TILE), 1)
        labels = jnp.zeros_like(lane)
        for t in range(count):
            labels = jnp.where(lane >= t * TILE, ref[base + t], labels)
        return labels

    count_ones = []
    for g in range(groups):
        ones = jnp.int32(0)
        for t in range(tiles):
            ones = ones + cd_ref[g * tiles + t]
        count_ones.append(ones)

    def places(j, way):
        lane = lax.broadcasted_iota(jnp.int32, (1, width), 1)
        offsets = [jnp.int32(0), jnp.int32(0)]
        for g in range(groups):
            counted = jnp.logical_and(g >= way, g < j)
            for label, count in ((0, tiles - count_ones[g]), (1, count_ones[g])):
                offsets[label] += jnp.where(counted, jnp.maximum(count - BASE, 0), 0)
        place = jnp.zeros_like(lane)
        pool_place = jnp.zeros_like(lane)
        ones = jnp.int32(0)
        for t in range(tiles):
            label = cd_ref[j * tiles + t]
            rank = jnp.where(label == 1, ones, t - ones)
            left_over = rank - BASE + jnp.where(label == 1, offsets[1], offsets[0])
            left_over = jnp.where(rank >= BASE, left_over, -tiles)
            place = jnp.where(lane >= t * TILE, lane + (rank - t) * TILE, place)
            pool_place = jnp.where(lane >= t * TILE, lane + (left_over - t) * TILE, pool_place)
            ones = ones + label
        return place, pool_place

    def fill(target, place):
        slot = lax.broadcasted_iota(jnp.int32, target.shape, 0)
        target[...] = jnp.where(slot == place, 1.0, 0.0).astype(jnp.bfloat16)

    for t in range(rows // TILE):
        pair_col[pl.ds(t * TILE, TILE), :] = jnp.full((TILE, 1), pair_ref[t], jnp.int32)
    fill(select, places(z, 0)[0])
    own_labels = lane_labels(cd_ref, z * tiles, tiles)

    @pl.loop(0, rows // BLOCK)
    def _(i):
        span = pl.ds(pl.multiple_of(i * BLOCK, BLOCK), BLOCK)
        kept = jnp.where(pair_col[span, :] == own_labels, amp_ref[span, :].astype(jnp.float32), 0.0)
        masked[span, :] = kept.astype(jnp.bfloat16)

    for h in range(HALVES):
        @pl.loop(0, rows // BLOCK)
        def _(i, h=h):
            span = pl.ds(pl.multiple_of(i * BLOCK, BLOCK), BLOCK)
            tile = lax.dot_general(
                select[pl.ds(h * half, half), :], masked[span, :],
                (((1,), (1,)), ((), ())), preferred_element_type=jnp.float32,
            )
            slabs[z, pl.ds(h * half, half), span] = tile.astype(jnp.bfloat16)

        @pl.when(z > 0)
        def _(h=h):
            send_amp(z, h, h, z - 1).start()

        @pl.when(z < last)
        def _(h=h):
            send_amp(z, h, 2 + h, z + 1).start()

    for w in range(groups):
        to_sib(w, 4).start()
    prior.start()

    def send_pool(way, h):
        span = pl.ds(h * (pooled // HALVES), pooled // HALVES)
        return pltpu.make_async_remote_copy(
            src_ref=pool_out.at[way, span, :],
            dst_ref=pool_in.at[way, span, :],
            send_sem=pool_send.at[way, h],
            recv_sem=pool_recv.at[way, h],
            device_id={"col": z + 1 - 2 * way},
            device_id_type=MESH,
        )

    @pl.loop(0, 2)
    def _(way):
        fill(pool_select, places(z, way)[1])

        @pl.loop(0, rows // BLOCK)
        def _(i):
            span = pl.ds(pl.multiple_of(i * BLOCK, BLOCK), BLOCK)
            pool_out[way, :, span] = lax.dot_general(
                pool_select[...], masked[span, :],
                (((1,), (1,)), ((), ())), preferred_element_type=jnp.float32,
            ).astype(jnp.bfloat16)

    @pl.when(z == 0)
    def _():
        for h in range(HALVES):
            send_pool(0, h).start()

    @pl.when(z == last)
    def _():
        for h in range(HALVES):
            send_pool(1, h).start()

    def pass_pool(way):
        for h in range(HALVES):
            span = pl.ds(h * (pooled // HALVES), pooled // HALVES)
            send_pool(way, h).wait_recv()
            pool_out[way, span, :] = pool_out[way, span, :] + pool_in[way, span, :]
            send_pool(way, h).start()

    pool_int[...] = jnp.zeros_like(pool_int)
    for g in range(groups):
        for t in range(tiles):
            cd_col[g, pl.ds(t * TILE, TILE), :] = jnp.full((TILE, 1), cd_ref[g * tiles + t], jnp.int32)
    ab_lane[...] = lane_labels(ab_ref, 0, columns // TILE)

    def pass_on(j, h, send_at, to):
        copy = send_amp(j, h, send_at, to)
        copy.wait_recv()
        copy.start()

    def pass_near(h):
        @pl.when(is_mid)
        def _():
            pass_on(z - 1, h, 4 + h, z + 1)
            pass_on(z + 1, h, 6 + h, z - 1)

    def pass_far(h):
        @pl.when(is_mid)
        def _():
            pass_on(far, h, 8 + h, far_to)

    def take_wave(w):
        recv_int(w, 0)
        fwd_y(w).start()
        recv_int(w, 1)
        fwd_x(w).start()

        @pl.when(w + 2 < groups)
        def _():
            own_x(w + 2).start()
            own_y(w + 2).start()

        to_sib(w, 5).start()
        to_sib(w, 6).start()

    def take_diag(w):
        recv_int(w, 2)
        recv_int(w, 3)
        to_sib(w, 7).start()

    def pair_up(w):
        j = order(w)
        way = (j > z).astype(jnp.int32)
        place, pool_place = places(j, way)
        fill(select, place)
        fill(pool_select, pool_place)

        @pl.loop(0, columns // cols)
        def _(c):
            at = pl.ds(pl.multiple_of(c * cols, cols), cols)
            part = jnp.where(cd_col[j] == ab_lane[:, at], panel[j, :, at].astype(jnp.float32), 0.0)
            part = part.astype(jnp.bfloat16)
            paired_int[:, at] = jnp.dot(
                select[...], part, preferred_element_type=jnp.float32
            ).astype(jnp.bfloat16)
            extra = jnp.dot(pool_select[...], part, preferred_element_type=jnp.float32)
            pool_int[way, :, at] = pool_int[way, :, at] + extra.astype(jnp.bfloat16)

    def wait_amp(w, h):
        @pl.when(jnp.logical_not(is_mid))
        def _():
            send_amp(order(w), h, 0, 0).wait_recv()

    def multiply(left_of, right, store):
        @pl.loop(0, rows // BLOCK)
        def _(i):
            span = pl.ds(pl.multiple_of(i * BLOCK, BLOCK), BLOCK)
            left = left_of(span)

            @pl.loop(0, columns // cols)
            def _(c):
                at = pl.ds(pl.multiple_of(c * cols, cols), cols)
                store(span, at, jnp.dot(left, right[:, at], preferred_element_type=jnp.float32))

    def put(span, at, value):
        total[span, at] = value

    def multiply_slab(w):
        multiply(lambda span: slabs[order(w), :, span].T, paired_int, add)

    def add(span, at, value):
        total[span, at] += value

    def finish(span, at, value):
        ladder = jnp.where(pair_col[span, :] == ab_lane[:, at], total[span, at] + value, 0.0)
        out_ref[span, at] = (res_v[span, at].astype(jnp.float32) + ladder).astype(jnp.bfloat16)

    pass_near(0)
    take_wave(0)
    pass_near(1)
    keep.wait()

    last_way = (z < 2).astype(jnp.int32)

    def multiply_pool(way, store):
        multiply(lambda span: pool_in[way, :, span].T, pool_int.at[way], store)

    @pl.loop(0, groups - 1)
    def _(w):
        take_wave(w + 1)

        @pl.when(w == 0)
        def _():
            pass_far(0)

        take_diag(w)
        for kind in (4, 5, 6, 7):
            recv_int(w, kind)

        @pl.when(w == 0)
        def _():
            multiply(lambda span: masked[span, :], panel.at[z], put)
            pass_far(1)

            @pl.when(is_mid)
            def _():
                pass_pool(1 - last_way)

        @pl.when(w > 0)
        def _():
            pair_up(w)

            @pl.when(jnp.logical_and(w == 2, is_mid))
            def _():
                pass_pool(last_way)

            for h in range(HALVES):
                wait_amp(w, h)
            multiply_slab(w)

    take_diag(last)
    for kind in (4, 5, 6, 7):
        recv_int(last, kind)
    pair_up(last)

    @pl.when(is_mid)
    def _():
        multiply_pool(1 - last_way, add)

    for h in range(HALVES):
        wait_amp(last, h)
    multiply_slab(last)
    prior.wait()

    @pl.when(jnp.logical_not(is_mid))
    def _():
        for h in range(HALVES):
            send_pool(last_way, h).wait_recv()

    multiply_pool(last_way, finish)

    for w in range(groups):
        for copy in (own_x, own_y, fwd_y, fwd_x):
            copy(w).wait_send()
        for kind in (4, 5, 6, 7):
            to_sib(w, kind).wait_send()
    for h in range(HALVES):
        @pl.when(z > 0)
        def _(h=h):
            send_amp(z, h, h, z - 1).wait_send()

        @pl.when(z < last)
        def _(h=h):
            send_amp(z, h, 2 + h, z + 1).wait_send()

        @pl.when(is_mid)
        def _(h=h):
            send_amp(z - 1, h, 4 + h, z + 1).wait_send()
            send_amp(z + 1, h, 6 + h, z - 1).wait_send()
            send_amp(far, h, 8 + h, far_to).wait_send()

    @pl.when(z < last)
    def _():
        for h in range(HALVES):
            send_pool(0, h).wait_send()

    @pl.when(z > 0)
    def _():
        for h in range(HALVES):
            send_pool(1, h).wait_send()


def call(slots, ident, pair_class, cd_class, ab_class, amplitudes, integrals, residual_in):
    rows, width = amplitudes.shape
    groups, _, columns = integrals.shape
    smem = pl.BlockSpec(memory_space=pltpu.SMEM)
    vmem = pl.BlockSpec(memory_space=pltpu.VMEM)
    hbm = pl.BlockSpec(memory_space=pl.ANY)
    packed = BASE * TILE
    pooled = slots * TILE
    return pl.pallas_call(
        kernel,
        out_shape=jax.ShapeDtypeStruct((rows, columns), jnp.bfloat16),
        in_specs=[smem] * 3 + [vmem] + [hbm] * 2,
        out_specs=vmem,
        scratch_shapes=[
            pltpu.VMEM((groups, packed, rows), jnp.bfloat16),
            pltpu.VMEM((2, pooled, rows), jnp.bfloat16),
            pltpu.VMEM((2, pooled, rows), jnp.bfloat16),
            pltpu.VMEM((2, pooled, columns), jnp.bfloat16),
            pltpu.VMEM((pooled, width), jnp.bfloat16),
            pltpu.VMEM((groups, width, columns), jnp.bfloat16),
            pltpu.VMEM((packed, columns), jnp.bfloat16),
            pltpu.VMEM((packed, width), jnp.bfloat16),
            pltpu.VMEM((rows, width), jnp.bfloat16),
            pltpu.VMEM((rows, columns), jnp.float32),
            pltpu.VMEM((rows, columns), jnp.bfloat16),
            pltpu.VMEM((rows, 1), jnp.int32),
            pltpu.VMEM((groups, width, 1), jnp.int32),
            pltpu.VMEM((1, columns), jnp.int32),
            pltpu.SemaphoreType.DMA((2,)),
            pltpu.SemaphoreType.DMA((8, groups)),
            pltpu.SemaphoreType.DMA((8, groups)),
            pltpu.SemaphoreType.DMA((10,)),
            pltpu.SemaphoreType.DMA((groups, HALVES)),
            pltpu.SemaphoreType.DMA((2, HALVES)),
            pltpu.SemaphoreType.DMA((2, HALVES)),
        ],
        compiler_params=pltpu.CompilerParams(
            collective_id=ident, has_side_effects=True, vmem_limit_bytes=56 * 1024 * 1024,
        ),
        cost_estimate=pl.CostEstimate(
            flops=2 * rows * width * groups * columns, bytes_accessed=2 * rows * columns * 3, transcendentals=0,
        ),
        name=f"ladder_{slots}",
    )(pair_class, cd_class, ab_class, amplitudes, integrals, residual_in)


def pool_sizes(groups, per_group):
    return (3, 4, 6, (groups - 1) * (per_group - BASE))


def choose(groups, per_group, cd_ref, which_ref):
    needed = jnp.int32(0)
    for label in (0, 1):
        left_over = []
        for g in range(groups):
            count = jnp.int32(0)
            for t in range(per_group):
                count += (cd_ref[g * per_group + t] == label).astype(jnp.int32)
            left_over.append(jnp.maximum(count - BASE, 0))
        ends = jnp.minimum(left_over[0], left_over[-1])
        needed = jnp.maximum(needed, sum(left_over) - ends)
    sizes = pool_sizes(groups, per_group)
    which_ref[0] = sum((needed > size).astype(jnp.int32) for size in sizes[:-1])


def paired(amplitudes, integrals, residual_in, pair_class, cd_class, ab_class):
    groups = integrals.shape[0]
    per_group = amplitudes.shape[1] // TILE
    smem = pl.BlockSpec(memory_space=pltpu.SMEM)
    which = pl.pallas_call(
        functools.partial(choose, groups, per_group),
        out_shape=jax.ShapeDtypeStruct((1,), jnp.int32),
        in_specs=[smem],
        out_specs=smem,
        name="choose",
    )(cd_class)
    branches = [functools.partial(call, size, ident) for ident, size in enumerate(pool_sizes(groups, per_group))]
    return lax.switch(which[0], branches, pair_class, cd_class, ab_class, amplitudes, integrals, residual_in)


def from_behind(value, axis, steps):
    count = lax.axis_size(axis)
    pairs = [(source, (source + steps) % count) for source in range(count)]
    return lax.ppermute(value, axis, pairs)


def ringed(amplitudes, integrals, residual_in, pair_class, cd_class, ab_class):
    pair_labels = jnp.repeat(pair_class, TILE)
    cd_labels = jnp.repeat(cd_class, TILE)
    ab_labels = jnp.repeat(ab_class, TILE)
    nothing = jnp.zeros((), jnp.bfloat16)
    slab_width = amplitudes.shape[1]

    def mask_amp(values, offset):
        labels = lax.dynamic_slice_in_dim(cd_labels, offset, values.shape[1])
        return jnp.where(pair_labels[:, None] == labels[None, :], values, nothing)

    def mask_int(values, offset):
        labels = lax.dynamic_slice_in_dim(cd_labels, offset, values.shape[0])
        return jnp.where(labels[:, None] == ab_labels[None, :], values, nothing)

    initial = residual_in.astype(jnp.float32)
    col_count = lax.axis_size("col")
    col_index = lax.axis_index("col")

    def contribute(ladder_sum, amp_slab, group_id):
        own_part = lax.dynamic_index_in_dim(integrals, group_id, 0, keepdims=False)
        int_panel = lax.all_gather(own_part, "row", axis=0, tiled=True)
        offset = group_id * slab_width
        return ladder_sum + jnp.dot(
            mask_amp(amp_slab, offset),
            mask_int(int_panel, offset),
            preferred_element_type=jnp.float32,
        )

    ladder_sum = contribute(initial, amplitudes, col_index)

    def advance(counter, state_pair):
        running, amp_slab = state_pair
        amp_slab = from_behind(amp_slab, "col", 1)
        group_id = (col_index - counter) % col_count
        return (contribute(running, amp_slab, group_id), amp_slab)

    ladder_sum, _ = lax.fori_loop(1, col_count, advance, (ladder_sum, amplitudes))
    return ladder_sum.astype(jnp.bfloat16)


def solution(mesh):
    local = paired if (mesh.shape["row"], mesh.shape["col"]) == (8, 4) else ringed
    return jax.shard_map(
        local,
        mesh=mesh,
        in_specs=(P("row", "col"), P(None, "row", "col"), P("row", "col"), P("row"), P(), P("col")),
        out_specs=P("row", "col"),
        check_vma=False,
    )
```
